128 devices in a mesh: head: 8 (over x, z_lo), tok: 16 (over z_hi, y, core).
Axes of the slice: x: 4, y: 4, z: 4 (z_hi: 2, z_lo: 2; z = z_hi * 2 + z_lo), core: 2. Of those that a mesh axis runs over, the one named last changes fastest.
Arguments:
- queries: bfloat16 [8192, 8192], P(('head', 'tok')), may hold values from -6 to 6
- keys: bfloat16 [8192, 8192], P(('head', 'tok')), may hold values from -6 to 6
- values: bfloat16 [8192, 8192], P(('head', 'tok')), may hold values from -6 to 6
- rates: bfloat16 [8192, 16], P(('head', 'tok')), may hold values from 0.049804688 to 1
- w_first: float32 [16, 512, 512], P('head'), may hold values from -0.25 to 0.25
- w_gate: float32 [16, 512, 512], P('head'), may hold values from -0.25 to 0.25
- w_second: float32 [16, 512, 512], P('head'), may hold values from -0.25 to 0.25
Outputs:
- mixed: bfloat16 [8192, 8192], P(('head', 'tok'))
- new_first: float32 [16, 512, 512], P('head')
- new_gate: float32 [16, 512, 512], P('head')
- new_second: float32 [16, 512, 512], P('head')
The draws below stay inside these ranges and needn't reach their ends.
All inputs are finite; a program needn't handle non-finite values.
Results may differ from the reference program's by a relative error of at most 0.0072.
Values may be sent and summed in bfloat16 or wider, within the bound.
A program may use at most 128 MiB of HBM per device.

```python
import math
import jax
import jax.numpy as jnp
from jax import lax

D = 8192
H = 16
DH = 512
ITERS = 3
TOKENS = 8192


def levels(own_key, shape, cuts, least, top_value):
    gain, own = 1.0, jax.random.fold_in(own_key, 6)
    for position, parts in cuts:
        steps = jnp.exp(jax.random.uniform(jax.random.fold_in(own, position), (parts,), jnp.float32, least / len(cuts), top_value / len(cuts)))
        gain = gain * jnp.repeat(steps, shape[position] // parts).reshape([-1 if axis == position else 1 for axis in range(len(shape))])
    return gain


def centred(stream_key, dims, scale, limit, cuts=(), held_as=jnp.bfloat16):
    array = jax.random.normal(stream_key, dims, jnp.float32) * scale
    if len(cuts) > 0:
        array = levels(stream_key, dims, cuts, -0.22, 0.18) * array
    return jnp.clip(array, min=-limit, max=limit).astype(held_as)


def setup_inputs(seed: int = 0) -> dict:
    key_of = jax.random.split(jax.random.key(seed), 8)
    queries = centred(key_of[0], (TOKENS, D), 1.0, 6.0, ((0, 128),))
    keys = centred(key_of[1], (TOKENS, D), 1.0, 6.0, ((0, 128),))
    values = centred(key_of[2], (TOKENS, D), 1.0, 6.0, ((0, 128),))
    rates = jnp.clip(jnp.exp(math.log(1.0) - 2.9996462 * jax.random.uniform(key_of[3], (TOKENS, H), jnp.float32) ** levels(key_of[3], (TOKENS, H), ((0, 128),), -0.2, 0.2)), 0.049804688, 1.0).astype(jnp.bfloat16)
    w_first = centred(key_of[4], (H, DH, DH), DH ** -0.5, 0.25, ((0, 8),), jnp.float32)
    w_gate = centred(key_of[5], (H, DH, DH), DH ** -0.5, 0.25, ((0, 8),), jnp.float32)
    w_second = centred(key_of[6], (H, DH, DH), DH ** -0.5, 0.25, ((0, 8),), jnp.float32)
    return dict(queries=queries, keys=keys, values=values, rates=rates, w_first=w_first, w_gate=w_gate, w_second=w_second)


def head_grads(keys_h, values_h, rates_h, weights):
    bf = jnp.bfloat16
    first = weights[0].astype(bf)
    gate = weights[1].astype(bf)
    second = weights[2].astype(bf)
    zone = jnp.dot(keys_h, first, preferred_element_type=jnp.float32)
    zthree = jnp.dot(keys_h, gate, preferred_element_type=jnp.float32)
    sigma = jax.nn.sigmoid(zone)
    active = zone * sigma
    hidden = (active * zthree).astype(bf)
    dpred = (-(rates_h.astype(jnp.float32)[:, None] * values_h.astype(jnp.float32))).astype(bf)
    gsecond = jnp.dot(hidden.T, dpred, preferred_element_type=jnp.float32)
    dhidden = jnp.dot(dpred, second.T, preferred_element_type=jnp.float32)
    dzone = (dhidden * zthree * sigma * (1.0 + zone * (1.0 - sigma))).astype(bf)
    dzthree = (dhidden * active).astype(bf)
    gfirst = jnp.dot(keys_h.T, dzone, preferred_element_type=jnp.float32)
    gthree = jnp.dot(keys_h.T, dzthree, preferred_element_type=jnp.float32)
    return jnp.stack([gfirst, gthree, gsecond], 0)

def newton(grads):
    norms = jnp.sqrt(lax.optimization_barrier(jnp.sum(grads * grads, axis=(-2, -1), keepdims=True)))
    state = grads / (norms + 1e-06)
    for step in range(ITERS):
        square = jnp.einsum('mij,mkj->mik', state, state, precision=lax.Precision.HIGHEST)
        state = 1.5 * state - 0.5 * jnp.einsum('mik,mkj->mij', square, state, precision=lax.Precision.HIGHEST)
    return state

def renew(weights, ortho):
    update = weights - ortho
    old_norm = jnp.sqrt(lax.optimization_barrier(jnp.sum(weights * weights, axis=-2, keepdims=True)) + 1e-06)
    new_norm = jnp.sqrt(lax.optimization_barrier(jnp.sum(update * update, axis=-2, keepdims=True)) + 1e-06)
    return update * (old_norm / new_norm)

def apply_head(queries_h, fresh):
    bf = jnp.bfloat16
    yone = jnp.dot(queries_h, fresh[0].astype(bf), preferred_element_type=jnp.float32)
    ythree = jnp.dot(queries_h, fresh[1].astype(bf), preferred_element_type=jnp.float32)
    qhidden = (jax.nn.silu(yone) * ythree).astype(bf)
    return jnp.dot(qhidden, fresh[2].astype(bf), preferred_element_type=jnp.float32).astype(bf)

def one_head(items):
    queries_h, keys_h, values_h, rates_h, weights = items
    grads = head_grads(keys_h, values_h, rates_h, weights)
    fresh = renew(weights, newton(grads))
    return (apply_head(queries_h, fresh), fresh)

def reference(queries, keys, values, rates, w_first, w_gate, w_second):

    def split(block):
        return jnp.transpose(block.reshape(TOKENS, H, DH), (1, 0, 2))
    weights = jnp.stack([w_first, w_gate, w_second], 1)
    outputs, fresh = lax.map(one_head, (split(queries), split(keys), split(values), rates.T, weights))
    mixed = jnp.transpose(outputs, (1, 0, 2)).reshape(TOKENS, H * DH)
    return (mixed, fresh[:, 0], fresh[:, 1], fresh[:, 2])
```

```python
import functools

import jax
import jax.numpy as jnp
from jax import lax
from jax.experimental import pallas as pl
from jax.experimental.pallas import tpu as pltpu
from jax.sharding import PartitionSpec as P

ITERS = 3
BF = jnp.bfloat16
F32 = jnp.float32
MESH = pl.DeviceIdType.MESH
GROUPS = 8
ROWS = 64
DH = 512
HALF = 256
SPAN = GROUPS * ROWS
TILE = 256
NT = (((1,), (1,)), ((), ()))
TN = (((0,), (0,)), ((), ()))
OFFSETS = ((1, 0), (3, 0), (0, 1), (2, 1), (2, 0), (1, 1), (3, 1))


def kernel(
    q_hbm, k_hbm, v_hbm, r_hbm, w1_hbm, w3_hbm, w2_hbm,
    mixed, out1, out3, out2,
    wv, vv, rv, dv, kin, din, qin, wb13, wb2, oldn, dz, hid,
    gs13, gs2, ry13, ry2, py13, py2, zs13, zs2, rz13, rz2, gg13, gg2,
    xs, xb, nb, qh, ov,
    load_sem, a2a_s, a2a_r, fw_s, fw_r, ry_s, ry_r, rz_s, rz_r,
    az_s, az_r, ay_s, ay_r, fg_s, fg_r, o_s, o_r,
):
    hi = lax.axis_index("head")
    tk = lax.axis_index("tok")
    x, zl = hi // 2, lax.rem(hi, 2)
    zh, y, c = tk // 8, lax.rem(tk // 2, 4), lax.rem(tk, 2)
    peers = [lax.rem(x + dx, 4) * 2 + lax.rem(zl + dz_, 2) for dx, dz_ in OFFSETS]
    ypeers = [zh * 8 + lax.rem(y + o, 4) * 2 + c for o in (1, 2, 3)]
    zpeer = (1 - zh) * 8 + y * 2 + c
    sib = zh * 8 + y * 2 + (1 - c)

    def remote(src, dst, s, r, **where):
        return pltpu.make_async_remote_copy(
            src_ref=src, dst_ref=dst, send_sem=s, recv_sem=r, device_id=where, device_id_type=MESH
        )

    def done(ref, sem):
        pltpu.make_async_copy(ref, ref, sem).wait()

    loads = [pltpu.make_async_copy(v_hbm, vv, load_sem.at[0]), pltpu.make_async_copy(r_hbm, rv, load_sem.at[1])]
    loads += [
        pltpu.make_async_copy(w, wv.at[m], load_sem.at[2 + m]) for m, w in enumerate((w1_hbm, w3_hbm, w2_hbm))
    ]
    for copy in loads:
        copy.start()

    barrier = pltpu.get_barrier_semaphore()
    for p in peers:
        pl.semaphore_signal(barrier, inc=1, device_id={"head": p}, device_id_type=MESH)
    for p in ypeers + [zpeer, sib]:
        pl.semaphore_signal(barrier, inc=1, device_id={"tok": p}, device_id_type=MESH)
    pl.semaphore_wait(barrier, len(peers) + 5)

    slot = pl.ds(pl.multiple_of(hi * ROWS, ROWS), ROWS)

    def columns(p, h):
        return pl.ds(pl.multiple_of((2 * p + h) * DH, DH), DH)

    def scatter(src, land, i, h):
        for p in peers:
            remote(src.at[:, columns(p, h)], land.at[slot], a2a_s.at[i], a2a_r.at[i], head=p).start()
        pltpu.make_async_copy(src.at[:, columns(hi, h)], land.at[slot], a2a_r.at[i]).start()

    def rate_values(h):
        rates = rv[...].astype(F32)
        for g in range(h, 2 * GROUPS, 2):
            cols = slice(g * DH, (g + 1) * DH)
            dv[:, cols] = (-(rates[:, g : g + 1] * vv[:, cols].astype(F32))).astype(BF)

    scatter(k_hbm, kin.at[0, c], 0, 0)
    loads[0].wait()
    loads[1].wait()
    rate_values(0)
    scatter(dv, din.at[0, c], 1, 0)
    scatter(k_hbm, kin.at[1, c], 2, 1)
    rate_values(1)
    scatter(dv, din.at[1, c], 3, 1)

    for copy in loads[2:]:
        copy.wait()
    half = pl.ds(pl.multiple_of(c * HALF, HALF), HALF)
    for h in range(2):
        wb13[h, :, :HALF] = wv[0, h, :, half].astype(BF)
        wb13[h, :, HALF:] = wv[1, h, :, half].astype(BF)
        wb2[h] = wv[2, h, half, :].astype(BF)
        for m in range(3):
            w = wv[m, h]
            oldn[3 * h + m] = jnp.broadcast_to(
                jnp.sqrt(jnp.sum(w * w, axis=0, keepdims=True) + 1e-06), (8, DH)
            )

    def forward(h):
        for i, buf in enumerate((kin, din)):
            done(buf.at[h, c], a2a_r.at[2 * h + i])
            remote(buf.at[h, c], buf.at[h, c], fw_s.at[2 * h + i], fw_r.at[2 * h + i], tok=sib).start()

    def hidden_grads(h, core):
        @pl.loop(0, SPAN // TILE)
        def _(step):
            at = pl.ds(pl.multiple_of(step * TILE, TILE), TILE)
            z = jnp.dot(kin[h, core, at, :], wb13[h], preferred_element_type=F32)
            dh = lax.dot_general(din[h, core, at, :], wb2[h], NT, preferred_element_type=F32)
            z1, z3 = z[:, :HALF], z[:, HALF:]
            sg = 1.0 / (1.0 + jnp.exp(-z1))
            act = z1 * sg
            hid[core, at, :] = (act * z3).astype(BF)
            dz[core, at, :HALF] = (dh * z3 * sg * (1.0 + z1 * (1.0 - sg))).astype(BF)
            dz[core, at, HALF:] = (dh * act).astype(BF)

    def send_y(src, land, rows, sems, i):
        for o, p in zip((1, 2, 3), ypeers):
            block = pl.ds(pl.multiple_of(lax.rem(y + o, 4) * rows, rows), rows)
            remote(src.at[block], land.at[pl.ds((3 - o) * rows, rows)], ry_s.at[i], ry_r.at[i], tok=p).start()

    def weight_grads(h):
        @pl.loop(0, 4)
        def _(j):
            cols = pl.ds(pl.multiple_of(j * 128, 128), 128)
            g = lax.dot_general(kin[h, 0, :, cols], dz[0], TN, preferred_element_type=F32)
            g += lax.dot_general(kin[h, 1, :, cols], dz[1], TN, preferred_element_type=F32)
            gs13[h, cols, :] = g.astype(BF)

        send_y(gs13.at[h], ry13.at[h], 128, ry_s, 2 * h)

        @pl.loop(0, 2)
        def _(j):
            cols = pl.ds(pl.multiple_of(j * 128, 128), 128)
            g = lax.dot_general(hid[0, :, cols], din[h, 0], TN, preferred_element_type=F32)
            g += lax.dot_general(hid[1, :, cols], din[h, 1], TN, preferred_element_type=F32)
            gs2[h, cols, :] = g.astype(BF)

        send_y(gs2.at[h], ry2.at[h], 64, ry_s, 2 * h + 1)

    mats = ((gs13, ry13, py13, zs13, rz13, gg13, 128), (gs2, ry2, py2, zs2, rz2, gg2, 64))

    def reduce_y(h):
        for i, (gs, ry, py, zs, rz, gg, n) in enumerate(mats):
            done(ry.at[h], ry_r.at[2 * h + i])
            own = pl.ds(pl.multiple_of(y * n, n), n)
            total = gs[h, own, :].astype(F32)
            for o in range(3):
                total += ry[h, pl.ds(o * n, n), :].astype(F32)
            py[h] = total
            zs[h] = py[h, pl.ds(pl.multiple_of((1 - zh) * (n // 2), n // 2), n // 2), :].astype(BF)
            remote(zs.at[h], rz.at[h], rz_s.at[2 * h + i], rz_r.at[2 * h + i], tok=zpeer).start()

    def gather(h):
        for i, (gs, ry, py, zs, rz, gg, n) in enumerate(mats):
            k = n // 2
            done(rz.at[h], rz_r.at[2 * h + i])
            total = py[h, pl.ds(pl.multiple_of(zh * k, k), k), :] + rz[h].astype(F32)
            own = pl.ds(pl.multiple_of(y * n + zh * k, k), k)
            gg[h, c, own, :] = total.astype(BF)
            view = gg.at[h, c, own]
            remote(view, view, az_s.at[2 * h + i], az_r.at[2 * h + i], tok=zpeer).start()
            for p in ypeers:
                remote(view, view, ay_s.at[2 * h + i], ay_r.at[2 * h + i], tok=p).start()
        for i, (gs, ry, py, zs, rz, gg, n) in enumerate(mats):
            k = n // 2
            other = pl.ds(pl.multiple_of(y * n + (1 - zh) * k, k), k)
            view = gg.at[h, c, other]
            done(view, az_r.at[2 * h + i])
            for p in ypeers:
                remote(view, view, ay_s.at[2 * h + i], ay_r.at[2 * h + i], tok=p).start()

    def share(h):
        for i, (gs, ry, py, zs, rz, gg, n) in enumerate(mats):
            done(gg.at[h, c, pl.ds(0, 3 * n)], ay_r.at[2 * h + i])
            remote(gg.at[h, c], gg.at[h, c], fg_s.at[2 * h + i], fg_r.at[2 * h + i], tok=sib).start()

    outs = (out1, out3, out2)

    def newton(h, m):
        def g_part(part):
            if m == 2:
                return gg2[h, part].astype(F32)
            return gg13[h, part, :, m * HALF : (m + 1) * HALF].astype(F32)

        squares = jnp.sum(g_part(0) ** 2) + jnp.sum(g_part(1) ** 2)
        scale = 1.0 / (jnp.sqrt(jnp.full((8, 128), squares, F32)) + 1e-06)
        scale = scale[:1, :1]
        for part in range(2):
            piece = g_part(part) * scale
            where = pl.ds(part * HALF, HALF)
            if m == 2:
                xs[where, :] = piece
                xb[0, where, :] = piece.astype(BF)
            else:
                xs[:, where] = piece
                xb[0, :, where] = piece.astype(BF)
        for step in range(ITERS):
            now, later = step % 2, (step + 1) % 2

            @pl.loop(0, DH // TILE)
            def _(j):
                at = pl.ds(pl.multiple_of(j * TILE, TILE), TILE)
                square = lax.dot_general(xb[now, at, :], xb[now], NT, preferred_element_type=F32)
                cube = jnp.dot(square.astype(BF), xb[now], preferred_element_type=F32)
                fresh = 1.5 * xs[at, :] - 0.5 * cube
                xs[at, :] = fresh
                if step < ITERS - 1:
                    xb[later, at, :] = fresh.astype(BF)

        update = wv[m, h] - xs[...]
        new_norm = jnp.sqrt(jnp.sum(update * update, axis=0, keepdims=True) + 1e-06)
        fresh = update * (oldn[3 * h + m, :1, :] / new_norm)
        outs[m][h] = fresh
        nb[m] = fresh.astype(BF)

    def apply(h):
        done(qin.at[h], a2a_r.at[4 + h])

        @pl.loop(0, SPAN // TILE)
        def _(step):
            at = pl.ds(pl.multiple_of(step * TILE, TILE), TILE)
            q = qin[h, at, :]
            y1 = jnp.dot(q, nb[0], preferred_element_type=F32)
            y3 = jnp.dot(q, nb[1], preferred_element_type=F32)
            qh[...] = (y1 * (1.0 / (1.0 + jnp.exp(-y1))) * y3).astype(BF)
            ov[h, at, :] = jnp.dot(qh[...], nb[2], preferred_element_type=F32).astype(BF)

        for p in peers:
            rows = pl.ds(pl.multiple_of(p * ROWS, ROWS), ROWS)
            remote(ov.at[h, rows], mixed.at[:, columns(hi, h)], o_s.at[h], o_r.at[h], head=p).start()
        pltpu.make_async_copy(ov.at[h, slot], mixed.at[:, columns(hi, h)], o_r.at[h]).start()

    forward(0)
    hidden_grads(0, c)
    for i, buf in enumerate((kin, din)):
        done(buf.at[0, 1 - c], fw_r.at[i])
    hidden_grads(0, 1 - c)
    weight_grads(0)

    forward(1)
    scatter(q_hbm, qin.at[0], 4, 0)
    scatter(q_hbm, qin.at[1], 5, 1)
    hidden_grads(1, c)
    reduce_y(0)
    for i, buf in enumerate((kin, din)):
        done(buf.at[1, 1 - c], fw_r.at[2 + i])
    hidden_grads(1, 1 - c)
    weight_grads(1)
    gather(0)
    reduce_y(1)
    share(0)
    gather(1)
    for i, gg in enumerate((gg13, gg2)):
        done(gg.at[0, 1 - c], fg_r.at[i])
    for m in range(3):
        newton(0, m)
    share(1)
    apply(0)
    for i, gg in enumerate((gg13, gg2)):
        done(gg.at[1, 1 - c], fg_r.at[2 + i])
    for m in range(3):
        newton(1, m)
    apply(1)

    sent = kin.at[0, 0, pl.ds(0, SPAN - ROWS)]
    for h in range(2):
        done(kin.at[0, 0], o_r.at[h])
        done(sent, o_s.at[h])
    for i in range(6):
        done(sent, a2a_s.at[i])
    for h in range(2):
        for i, (gs, ry, py, zs, rz, gg, n) in enumerate(mats):
            j = 2 * h + i
            done(kin.at[0, 0], fw_s.at[j])
            done(gs.at[h, pl.ds(0, 3 * n)], ry_s.at[j])
            done(zs.at[h], rz_s.at[j])
            done(zs.at[h], az_s.at[j])
            done(gg.at[h, c, pl.ds(0, 3 * n)], ay_s.at[j])
            done(gg.at[h, c], fg_s.at[j])


def on_device(queries, keys, values, rates, w_first, w_gate, w_second):
    any_spec = pl.BlockSpec(memory_space=pl.ANY)
    vmem_spec = pl.BlockSpec(memory_space=pltpu.VMEM)
    dma = pltpu.SemaphoreType.DMA
    weights = jax.ShapeDtypeStruct(w_first.shape, F32)
    vm = pltpu.VMEM
    return pl.pallas_call(
        kernel,
        out_shape=(jax.ShapeDtypeStruct(queries.shape, BF), weights, weights, weights),
        in_specs=[any_spec] * 7,
        out_specs=(any_spec, vmem_spec, vmem_spec, vmem_spec),
        scratch_shapes=[
            vm((3, 2, DH, DH), F32),
            vm(values.shape, BF),
            vm(rates.shape, BF),
            vm(values.shape, BF),
            vm((2, 2, SPAN, DH), BF),
            vm((2, 2, SPAN, DH), BF),
            vm((2, SPAN, DH), BF),
            vm((2, DH, DH), BF),
            vm((2, HALF, DH), BF),
            vm((6, 8, DH), F32),
            vm((2, SPAN, DH), BF),
            vm((2, SPAN, HALF), BF),
            vm((2, DH, DH), BF),
            vm((2, HALF, DH), BF),
            vm((2, 384, DH), BF),
            vm((2, 192, DH), BF),
            vm((2, 128, DH), F32),
            vm((2, 64, DH), F32),
            vm((2, 64, DH), BF),
            vm((2, 32, DH), BF),
            vm((2, 64, DH), BF),
            vm((2, 32, DH), BF),
            vm((2, 2, DH, DH), BF),
            vm((2, 2, HALF, DH), BF),
            vm((DH, DH), F32),
            vm((2, DH, DH), BF),
            vm((3, DH, DH), BF),
            vm((TILE, DH), BF),
            vm((2, SPAN, DH), BF),
            dma((5,)), dma((6,)), dma((6,)), dma((4,)), dma((4,)), dma((4,)), dma((4,)),
            dma((4,)), dma((4,)), dma((4,)), dma((4,)), dma((4,)), dma((4,)), dma((4,)),
            dma((4,)), dma((2,)), dma((2,)),
        ],
        compiler_params=pltpu.CompilerParams(
            collective_id=0, has_side_effects=True, vmem_limit_bytes=56 * 1024 * 1024
        ),
        name="layer",
    )(queries, keys, values, rates, w_first, w_gate, w_second)


def solution(mesh):
    placed = (
        P(("head", "tok"), None),
        P(("head", "tok"), None),
        P(("head", "tok"), None),
        P(("head", "tok"), None),
        P("head", None, None),
        P("head", None, None),
        P("head", None, None),
    )
    return jax.shard_map(
        on_device,
        mesh=mesh,
        in_specs=placed,
        out_specs=(
            P(("head", "tok"), None),
            P("head", None, None),
            P("head", None, None),
            P("head", None, None),
        ),
        check_vma=False,
    )
```

```python
import functools

import jax
import jax.numpy as jnp
from jax import lax
from jax.experimental import pallas as pl
from jax.experimental.pallas import tpu as pltpu
from jax.sharding import PartitionSpec as P

ITERS = 3
BF = jnp.bfloat16
F32 = jnp.float32
MESH = pl.DeviceIdType.MESH
GROUPS = 8
ROWS = 64
DH = 512
HALF = 256
VMEM_BYTES = 56 * 1024 * 1024
SPAN = GROUPS * ROWS
TILE = 256
NT = (((1,), (1,)), ((), ()))
TN = (((0,), (0,)), ((), ()))
OFFSETS = ((2, 1), (2, 0), (1, 1), (3, 1), (1, 0), (3, 0), (0, 1))
BACK = tuple(OFFSETS.index(((4 - dx) % 4, dz)) for dx, dz in OFFSETS)
OWN = len(OFFSETS)


def kernel(
    q_hbm, k_hbm, v_hbm, r_hbm, w1_hbm, w3_hbm, w2_hbm,
    mixed, out1, out3, out2,
    wv, vv, rv, dv, kin, din, qin, wb13, wb2, oldn, dz, hid,
    gs13, gs2, ry13, ry2, py13, py2, zs13, zs2, rz13, rz2, gg13, gg2,
    xs, xb, nb, qh, ov, nf,
    load_sem, a2a_s, a2a_r, fw_s, fw_r, ry_s, ry_r, rz_s, rz_r,
    az_s, az_r, ay_s, ay_r, fg_s, fg_r, o_s, o_r, nf_sem,
):
    hi = lax.axis_index("head")
    tk = lax.axis_index("tok")
    x, zl = hi // 2, lax.rem(hi, 2)
    zh, y, c = tk // 8, lax.rem(tk // 2, 4), lax.rem(tk, 2)
    peers = [lax.rem(x + dx, 4) * 2 + lax.rem(zl + dz_, 2) for dx, dz_ in OFFSETS]
    ypeers = [zh * 8 + lax.rem(y + o, 4) * 2 + c for o in (1, 2, 3)]
    zpeer = (1 - zh) * 8 + y * 2 + c
    sib = zh * 8 + y * 2 + (1 - c)

    def remote(src, dst, s, r, **where):
        return pltpu.make_async_remote_copy(
            src_ref=src, dst_ref=dst, send_sem=s, recv_sem=r, device_id=where, device_id_type=MESH
        )

    pending = {}

    def done(name, i):
        ref, sem = pending.pop((name, i))
        pltpu.make_async_copy(ref, ref, sem).wait()

    def track(name, i, sent, arriving, send_sems, recv_sems):
        pending[name + "_s", i] = (sent, send_sems.at[i])
        pending[name, i] = (arriving, recv_sems.at[i])

    loads = [pltpu.make_async_copy(v_hbm, vv, load_sem.at[0]), pltpu.make_async_copy(r_hbm, rv, load_sem.at[1])]
    loads += [
        pltpu.make_async_copy(w, wv.at[m], load_sem.at[2 + m]) for m, w in enumerate((w1_hbm, w3_hbm, w2_hbm))
    ]
    for copy in loads:
        copy.start()

    barrier = pltpu.get_barrier_semaphore()
    for p in peers:
        pl.semaphore_signal(barrier, inc=1, device_id={"head": p}, device_id_type=MESH)
    for p in ypeers + [zpeer, sib]:
        pl.semaphore_signal(barrier, inc=1, device_id={"tok": p}, device_id_type=MESH)
    pl.semaphore_wait(barrier, len(peers) + 5)

    def slot(i):
        return pl.ds(i * ROWS, ROWS)

    def columns(p, h):
        return pl.ds(pl.multiple_of((2 * p + h) * DH, DH), DH)

    def scatter(src, land, i, h):
        for p, b in zip(peers, BACK):
            remote(src.at[:, columns(p, h)], land.at[slot(b)], a2a_s.at[i], a2a_r.at[i], head=p).start()
        pltpu.make_async_copy(src.at[:, columns(hi, h)], land.at[slot(OWN)], a2a_r.at[i]).start()
        track("a2a", i, land.at[pl.ds(0, SPAN - ROWS)], land, a2a_s, a2a_r)

    def rate_values(h):
        rates = rv[...].astype(F32).T
        for g in range(h, 2 * GROUPS, 2):
            cols = slice(g * DH, (g + 1) * DH)
            dv[:, cols] = (-(rates[:, g : g + 1] * vv[:, cols].astype(F32))).astype(BF)

    scatter(k_hbm, kin.at[0, c], 0, 0)
    loads[0].wait()
    loads[1].wait()
    rate_values(0)
    scatter(dv, din.at[0, c], 1, 0)
    scatter(k_hbm, kin.at[1, c], 2, 1)
    rate_values(1)
    scatter(dv, din.at[1, c], 3, 1)

    for copy in loads[2:]:
        copy.wait()
    half = pl.ds(pl.multiple_of(c * HALF, HALF), HALF)
    for h in range(2):
        wb13[h, :, :HALF] = wv[0, h, :, half].astype(BF)
        wb13[h, :, HALF:] = wv[1, h, :, half].astype(BF)
        wb2[h] = wv[2, h, half, :].astype(BF)
        for m in range(3):
            w = wv[m, h]
            oldn[3 * h + m] = jnp.broadcast_to(
                jnp.sqrt(jnp.sum(w * w, axis=0, keepdims=True) + 1e-06), (8, DH)
            )

    def forward(h):
        for i, buf in enumerate((kin, din)):
            j = 2 * h + i
            done("a2a", j)
            remote(buf.at[h, c], buf.at[h, c], fw_s.at[j], fw_r.at[j], tok=sib).start()
            track("fw", j, buf.at[h, c], buf.at[h, 1 - c], fw_s, fw_r)

    def hidden_grads(h, core):
        @pl.loop(0, SPAN // TILE)
        def _(step):
            at = pl.ds(pl.multiple_of(step * TILE, TILE), TILE)
            z = jnp.dot(kin[h, core, at, :], wb13[h], preferred_element_type=F32)
            dh = lax.dot_general(din[h, core, at, :], wb2[h], NT, preferred_element_type=F32)
            z1, z3 = z[:, :HALF], z[:, HALF:]
            sg = 1.0 / (1.0 + jnp.exp(-z1))
            act = z1 * sg
            hid[core, at, :] = (act * z3).astype(BF)
            dz[core, at, :HALF] = (dh * z3 * sg * (1.0 + z1 * (1.0 - sg))).astype(BF)
            dz[core, at, HALF:] = (dh * act).astype(BF)

    def send_y(src, land, rows, sems, i):
        for o, p in zip((1, 2, 3), ypeers):
            block = pl.ds(pl.multiple_of(lax.rem(y + o, 4) * rows, rows), rows)
            remote(src.at[block], land.at[pl.ds((3 - o) * rows, rows)], ry_s.at[i], ry_r.at[i], tok=p).start()
        track("ry", i, src.at[pl.ds(0, 3 * rows)], land, ry_s, ry_r)

    def weight_grads(h):
        g = lax.dot_general(kin[h, 0], dz[0], TN, preferred_element_type=F32)
        g += lax.dot_general(kin[h, 1], dz[1], TN, preferred_element_type=F32)
        gs13[h] = g.astype(BF)
        send_y(gs13.at[h], ry13.at[h], 128, ry_s, 2 * h)
        g = lax.dot_general(hid[0], din[h, 0], TN, preferred_element_type=F32)
        g += lax.dot_general(hid[1], din[h, 1], TN, preferred_element_type=F32)
        gs2[h] = g.astype(BF)
        send_y(gs2.at[h], ry2.at[h], 64, ry_s, 2 * h + 1)

    mats = ((gs13, ry13, py13, zs13, rz13, gg13, 128), (gs2, ry2, py2, zs2, rz2, gg2, 64))

    def reduce_y(h):
        for i, (gs, ry, py, zs, rz, gg, n) in enumerate(mats):
            done("ry", 2 * h + i)
            own = pl.ds(pl.multiple_of(y * n, n), n)
            total = gs[h, own, :].astype(F32)
            for o in range(3):
                total += ry[h, pl.ds(o * n, n), :].astype(F32)
            py[h] = total
            zs[h] = py[h, pl.ds(pl.multiple_of((1 - zh) * (n // 2), n // 2), n // 2), :].astype(BF)
            remote(zs.at[h], rz.at[h], rz_s.at[2 * h + i], rz_r.at[2 * h + i], tok=zpeer).start()
            track("rz", 2 * h + i, zs.at[h], rz.at[h], rz_s, rz_r)

    def gather(h):
        for i, (gs, ry, py, zs, rz, gg, n) in enumerate(mats):
            k = n // 2
            done("rz", 2 * h + i)
            total = py[h, pl.ds(pl.multiple_of(zh * k, k), k), :] + rz[h].astype(F32)
            own = pl.ds(pl.multiple_of(y * n + zh * k, k), k)
            gg[h, c, own, :] = total.astype(BF)
            view = gg.at[h, c, own]
            other = pl.ds(pl.multiple_of(y * n + (1 - zh) * k, k), k)
            remote(view, view, az_s.at[2 * h + i], az_r.at[2 * h + i], tok=zpeer).start()
            track("az", 2 * h + i, view, gg.at[h, c, other], az_s, az_r)
            for p in ypeers:
                remote(view, view, ay_s.at[2 * h + i], ay_r.at[2 * h + i], tok=p).start()

    def pass_on(h):
        for i, (gs, ry, py, zs, rz, gg, n) in enumerate(mats):
            k = n // 2
            other = pl.ds(pl.multiple_of(y * n + (1 - zh) * k, k), k)
            view = gg.at[h, c, other]
            done("az", 2 * h + i)
            for p in ypeers:
                remote(view, view, ay_s.at[2 * h + i], ay_r.at[2 * h + i], tok=p).start()
            three = gg.at[h, c, pl.ds(0, 3 * n)]
            track("ay", 2 * h + i, three, three, ay_s, ay_r)

    def share(h):
        for i, (gs, ry, py, zs, rz, gg, n) in enumerate(mats):
            j = 2 * h + i
            done("ay", j)
            remote(gg.at[h, c], gg.at[h, c], fg_s.at[j], fg_r.at[j], tok=sib).start()
            track("fg", j, gg.at[h, c], gg.at[h, 1 - c], fg_s, fg_r)

    outs = (out1, out3, out2)

    def newton(h, m):
        def g_part(part):
            if m == 2:
                return gg2[h, part].astype(F32)
            return gg13[h, part, :, m * HALF : (m + 1) * HALF].astype(F32)

        squares = jnp.sum(g_part(0) ** 2) + jnp.sum(g_part(1) ** 2)
        scale = 1.0 / (jnp.sqrt(jnp.full((8, 128), squares, F32)) + 1e-06)
        scale = scale[:1, :1]
        for part in range(2):
            piece = g_part(part) * scale
            where = pl.ds(part * HALF, HALF)
            if m == 2:
                xs[where, :] = piece
                xb[0, where, :] = piece.astype(BF)
            else:
                xs[:, where] = piece
                xb[0, :, where] = piece.astype(BF)
        for step in range(ITERS):
            now, later = step % 2, (step + 1) % 2

            square = lax.dot_general(xb[now], xb[now], NT, preferred_element_type=F32)
            cube = jnp.dot(square.astype(BF), xb[now], preferred_element_type=F32)
            fresh = 1.5 * xs[...] - 0.5 * cube
            xs[...] = fresh
            if step < ITERS - 1:
                xb[later] = fresh.astype(BF)

        update = wv[m, h] - xs[...]
        new_norm = jnp.sqrt(jnp.sum(update * update, axis=0, keepdims=True) + 1e-06)
        fresh = update * (oldn[3 * h + m, :1, :] / new_norm)
        nf[h, m] = fresh
        pltpu.make_async_copy(nf.at[h, m], outs[m].at[h], nf_sem.at[3 * h + m]).start()
        pending["nf_s", 3 * h + m] = (nf.at[h, m], nf_sem.at[3 * h + m])
        nb[m] = fresh.astype(BF)

    def apply(h):
        done("a2a", 4 + h)

        for tile in range(SPAN // TILE):
            at = pl.ds(tile * TILE, TILE)
            q = qin[h, at, :]
            y1 = jnp.dot(q, nb[0], preferred_element_type=F32)
            y3 = jnp.dot(q, nb[1], preferred_element_type=F32)
            qh[...] = (y1 * (1.0 / (1.0 + jnp.exp(-y1))) * y3).astype(BF)
            ov[h, at, :] = jnp.dot(qh[...], nb[2], preferred_element_type=F32).astype(BF)
            for i in range(tile * TILE // ROWS, (tile + 1) * TILE // ROWS):
                land = mixed.at[:, columns(hi, h)]
                if i == OWN:
                    pltpu.make_async_copy(ov.at[h, slot(i)], land, o_r.at[h]).start()
                else:
                    remote(ov.at[h, slot(i)], land, o_s.at[h], o_r.at[h], head=peers[i]).start()
        track("out", h, ov.at[h, pl.ds(0, SPAN - ROWS)], ov.at[h], o_s, o_r)

    def arrived(name, h):
        done(name, 2 * h)
        done(name, 2 * h + 1)

    steps = [
        lambda: forward(0),
        lambda: hidden_grads(0, c),
        lambda: arrived("fw", 0),
        lambda: hidden_grads(0, 1 - c),
        lambda: weight_grads(0),
        lambda: forward(1),
        lambda: hidden_grads(1, c),
        lambda: arrived("fw", 1),
        lambda: hidden_grads(1, 1 - c),
        lambda: weight_grads(1),
        lambda: scatter(q_hbm, qin.at[0], 4, 0),
        lambda: scatter(q_hbm, qin.at[1], 5, 1),
        lambda: reduce_y(0),
        lambda: gather(0),
        lambda: pass_on(0),
        lambda: reduce_y(1),
        lambda: gather(1),
        lambda: pass_on(1),
        lambda: share(0),
        lambda: arrived("fg", 0),
        lambda: newton(0, 0),
        lambda: newton(0, 1),
        lambda: newton(0, 2),
        lambda: share(1),
        lambda: apply(0),
        lambda: arrived("fg", 1),
        lambda: newton(1, 0),
        lambda: newton(1, 1),
        lambda: newton(1, 2),
        lambda: apply(1),
    ]
    for step in steps:
        step()

    for key in sorted(pending, key=lambda key: (key[0].endswith("_s"), key)):
        done(*key)


def hand_out(*refs):
    count = len(refs) // 2
    copies = [pltpu.make_async_copy(refs[i], refs[count + i], refs[-1].at[i]) for i in range(count)]
    for copy in copies:
        copy.start()
    for copy in copies:
        copy.wait()


def on_device(queries, keys, values, rates, w_first, w_gate, w_second):
    any_spec = pl.BlockSpec(memory_space=pl.ANY)
    dma = pltpu.SemaphoreType.DMA
    weights = jax.ShapeDtypeStruct(w_first.shape, F32)
    vm = pltpu.VMEM
    results = pl.pallas_call(
        kernel,
        out_shape=(jax.ShapeDtypeStruct(queries.shape, BF), weights, weights, weights),
        in_specs=[any_spec] * 7,
        out_specs=[any_spec] * 4,
        scratch_shapes=[
            vm((3, 2, DH, DH), F32),
            vm(values.shape, BF),
            vm(rates.shape[::-1], BF),
            vm(values.shape, BF),
            vm((2, 2, SPAN, DH), BF),
            vm((2, 2, SPAN, DH), BF),
            vm((2, SPAN, DH), BF),
            vm((2, DH, DH), BF),
            vm((2, HALF, DH), BF),
            vm((6, 8, DH), F32),
            vm((2, SPAN, DH), BF),
            vm((2, SPAN, HALF), BF),
            vm((2, DH, DH), BF),
            vm((2, HALF, DH), BF),
            vm((2, 384, DH), BF),
            vm((2, 192, DH), BF),
            vm((2, 128, DH), F32),
            vm((2, 64, DH), F32),
            vm((2, 64, DH), BF),
            vm((2, 32, DH), BF),
            vm((2, 64, DH), BF),
            vm((2, 32, DH), BF),
            vm((2, 2, DH, DH), BF),
            vm((2, 2, HALF, DH), BF),
            vm((DH, DH), F32),
            vm((2, DH, DH), BF),
            vm((3, DH, DH), BF),
            vm((TILE, DH), BF),
            vm((2, SPAN, DH), BF),
            vm((2, 3, DH, DH), F32),
            dma((5,)), dma((6,)), dma((6,)), dma((4,)), dma((4,)), dma((4,)), dma((4,)),
            dma((4,)), dma((4,)), dma((4,)), dma((4,)), dma((4,)), dma((4,)), dma((4,)),
            dma((4,)), dma((2,)), dma((2,)), dma((6,)),
        ],
        compiler_params=pltpu.CompilerParams(
            collective_id=0, has_side_effects=True, vmem_limit_bytes=VMEM_BYTES
        ),
        name="layer",
    )(queries, keys, values, rates.T, w_first, w_gate, w_second)
    return pl.pallas_call(
        hand_out,
        out_shape=(jax.ShapeDtypeStruct(queries.shape, BF), weights, weights, weights),
        in_specs=[any_spec] * 4,
        out_specs=[any_spec] * 4,
        scratch_shapes=[dma((4,))],
        name="hand_out",
    )(*results)


def solution(mesh):
    placed = (
        P(("head", "tok"), None),
        P(("head", "tok"), None),
        P(("head", "tok"), None),
        P(("head", "tok"), None),
        P("head", None, None),
        P("head", None, None),
        P("head", None, None),
    )
    return jax.shard_map(
        on_device,
        mesh=mesh,
        in_specs=placed,
        out_specs=(
            P(("head", "tok"), None),
            P("head", None, None),
            P("head", None, None),
            P("head", None, None),
        ),
        check_vma=False,
    )
```

```python
import functools

import jax
import jax.numpy as jnp
from jax import lax
from jax.experimental import pallas as pl
from jax.experimental.pallas import tpu as pltpu
from jax.sharding import PartitionSpec as P

ITERS = 3
BF = jnp.bfloat16
F32 = jnp.float32
MESH = pl.DeviceIdType.MESH
GROUPS = 8
ROWS = 64
DH = 512
HALF = 256
VMEM_BYTES = 56 * 1024 * 1024
SPAN = GROUPS * ROWS
TILE = 256
NT = (((1,), (1,)), ((), ()))
TN = (((0,), (0,)), ((), ()))
OFFSETS = ((2, 1), (2, 0), (1, 1), (3, 1), (1, 0), (3, 0), (0, 1))
BACK = tuple(OFFSETS.index(((4 - dx) % 4, dz)) for dx, dz in OFFSETS)
OWN = len(OFFSETS)


def kernel(
    q_hbm, k_hbm, v_hbm, r_hbm, w1_hbm, w3_hbm, w2_hbm,
    mixed, out1, out3, out2,
    wv, vv, rv, dv, kin, din, qin, wb13, wb2, oldn, dz, hid,
    gs13, gs2, ra13, ra2, rb13, rb2, ry13, ry2, py13, py2, zs13, zs2, rz13, rz2, gg13, gg2,
    xs, xb, xf, nb, qh, ov, nf,
    load_sem, a2a_s, a2a_r, fw_s, fw_r, ra_r, ry_s, ry_r, rz_s, rz_r,
    az_s, az_r, ay_s, ay_r, au_r, ad_r, fg_s, fg_r, xf_s, xf_r, o_s, o_r, nf_sem,
):
    hi = lax.axis_index("head")
    tk = lax.axis_index("tok")
    x, zl = hi // 2, lax.rem(hi, 2)
    zh, y, c = tk // 8, lax.rem(tk // 2, 4), lax.rem(tk, 2)
    peers = [lax.rem(x + dx, 4) * 2 + lax.rem(zl + dz_, 2) for dx, dz_ in OFFSETS]
    up, down = [zh * 8 + lax.rem(y + o, 4) * 2 + c for o in (1, 3)]
    zpeer = (1 - zh) * 8 + y * 2 + c
    sib = zh * 8 + y * 2 + (1 - c)

    def remote(src, dst, s, r, **where):
        return pltpu.make_async_remote_copy(
            src_ref=src, dst_ref=dst, send_sem=s, recv_sem=r, device_id=where, device_id_type=MESH
        )

    pending = {}

    def done(name, i):
        ref, sem = pending.pop((name, i))
        pltpu.make_async_copy(ref, ref, sem).wait()

    def track(name, i, sent, arriving, send_sems, recv_sems):
        pending[name + "_s", i] = (sent, send_sems.at[i])
        pending[name, i] = (arriving, recv_sems.at[i])

    loads = [pltpu.make_async_copy(v_hbm, vv, load_sem.at[0]), pltpu.make_async_copy(r_hbm, rv, load_sem.at[1])]
    loads += [
        pltpu.make_async_copy(w, wv.at[m], load_sem.at[2 + m]) for m, w in enumerate((w1_hbm, w3_hbm, w2_hbm))
    ]
    for copy in loads:
        copy.start()

    barrier = pltpu.get_barrier_semaphore()
    for p in peers:
        pl.semaphore_signal(barrier, inc=1, device_id={"head": p}, device_id_type=MESH)
    for p in (up, down, zpeer, sib):
        pl.semaphore_signal(barrier, inc=1, device_id={"tok": p}, device_id_type=MESH)
    pl.semaphore_wait(barrier, len(peers) + 4)

    def slot(i):
        return pl.ds(i * ROWS, ROWS)

    def columns(p, h):
        return pl.ds(pl.multiple_of((2 * p + h) * DH, DH), DH)

    def scatter(src, land, i, h):
        for p, b in zip(peers, BACK):
            remote(src.at[:, columns(p, h)], land.at[slot(b)], a2a_s.at[i], a2a_r.at[i], head=p).start()
        pltpu.make_async_copy(src.at[:, columns(hi, h)], land.at[slot(OWN)], a2a_r.at[i]).start()
        track("a2a", i, land.at[pl.ds(0, SPAN - ROWS)], land, a2a_s, a2a_r)

    def rate_values(h):
        rates = rv[...].astype(F32).T
        for g in range(h, 2 * GROUPS, 2):
            cols = slice(g * DH, (g + 1) * DH)
            dv[:, cols] = (-(rates[:, g : g + 1] * vv[:, cols].astype(F32))).astype(BF)

    scatter(k_hbm, kin.at[0, c], 0, 0)
    loads[0].wait()
    loads[1].wait()
    rate_values(0)
    scatter(dv, din.at[0, c], 1, 0)
    scatter(k_hbm, kin.at[1, c], 2, 1)
    rate_values(1)
    scatter(dv, din.at[1, c], 3, 1)

    for copy in loads[2:]:
        copy.wait()
    half = pl.ds(pl.multiple_of(c * HALF, HALF), HALF)
    for h in range(2):
        wb13[h, :, :HALF] = wv[0, h, :, half].astype(BF)
        wb13[h, :, HALF:] = wv[1, h, :, half].astype(BF)
        wb2[h] = wv[2, h, half, :].astype(BF)
        for m in range(3):
            w = wv[m, h]
            oldn[h, m] = jnp.broadcast_to(
                jnp.sqrt(jnp.sum(w * w, axis=0, keepdims=True) + 1e-06), (8, DH)
            )

    def forward(h):
        for i, buf in enumerate((kin, din)):
            j = 2 * h + i
            done("a2a", j)
            remote(buf.at[h, c], buf.at[h, c], fw_s.at[j], fw_r.at[j], tok=sib).start()
            track("fw", j, buf.at[h, c], buf.at[h, 1 - c], fw_s, fw_r)

    def hidden_grads(h, core):
        @pl.loop(0, SPAN // TILE)
        def _(step):
            at = pl.ds(pl.multiple_of(step * TILE, TILE), TILE)
            z = jnp.dot(kin[h, core, at, :], wb13[h], preferred_element_type=F32)
            dh = lax.dot_general(din[h, core, at, :], wb2[h], NT, preferred_element_type=F32)
            z1, z3 = z[:, :HALF], z[:, HALF:]
            sg = 1.0 / (1.0 + jnp.exp(-z1))
            act = z1 * sg
            hid[core, at, :] = (act * z3).astype(BF)
            dz[core, at, :HALF] = (dh * z3 * sg * (1.0 + z1 * (1.0 - sg))).astype(BF)
            dz[core, at, HALF:] = (dh * act).astype(BF)

    def block(j, rows, start=0, count=None):
        return pl.ds(pl.multiple_of(lax.rem(y + j, 4) * rows + start, 16), count or rows)

    def send_y(gs, ra, ry, n, i):
        k = n // 2
        remote(gs.at[block(2, n, 0, k)], ra.at[0], ry_s.at[i], ra_r.at[i], tok=up).start()
        remote(gs.at[block(2, n, k, k)], ra.at[1], ry_s.at[i], ra_r.at[i], tok=down).start()
        remote(gs.at[block(1, n, k, k)], ry.at[0], ry_s.at[i], ry_r.at[i], tok=up).start()
        remote(gs.at[block(3, n, 0, k)], ry.at[1], ry_s.at[i], ry_r.at[i], tok=down).start()
        pending["ra", i] = (ra, ra_r.at[i])

    def weight_grads(h):
        g = lax.dot_general(kin[h, 0], dz[0], TN, preferred_element_type=F32)
        g += lax.dot_general(kin[h, 1], dz[1], TN, preferred_element_type=F32)
        gs13[h] = g.astype(BF)
        send_y(gs13.at[h], ra13.at[h], ry13.at[h], 128, 2 * h)
        g = lax.dot_general(hid[0], din[h, 0], TN, preferred_element_type=F32)
        g += lax.dot_general(hid[1], din[h, 1], TN, preferred_element_type=F32)
        gs2[h] = g.astype(BF)
        send_y(gs2.at[h], ra2.at[h], ry2.at[h], 64, 2 * h + 1)

    mats = (
        (gs13, ra13, rb13, ry13, py13, zs13, rz13, gg13, 128),
        (gs2, ra2, rb2, ry2, py2, zs2, rz2, gg2, 64),
    )

    def relay_y(h):
        for i, (gs, ra, rb, ry, py, zs, rz, gg, n) in enumerate(mats):
            j, k = 2 * h + i, n // 2
            done("ra", j)
            rb[h, 0] = (gs[h, block(1, n, 0, k), :].astype(F32) + ra[h, 0].astype(F32)).astype(BF)
            rb[h, 1] = (gs[h, block(3, n, k, k), :].astype(F32) + ra[h, 1].astype(F32)).astype(BF)
            remote(rb.at[h, 0], ry.at[h, 2], ry_s.at[j], ry_r.at[j], tok=up).start()
            remote(rb.at[h, 1], ry.at[h, 3], ry_s.at[j], ry_r.at[j], tok=down).start()
            track("ry", j, gs.at[h, pl.ds(0, 3 * n)], ry.at[h], ry_s, ry_r)

    def reduce_y(h):
        for i, (gs, ra, rb, ry, py, zs, rz, gg, n) in enumerate(mats):
            j, k = 2 * h + i, n // 2
            done("ry", j)
            own = gs[h, block(0, n), :].astype(F32)
            py[h, :k, :] = own[:k] + (ry[h, 2].astype(F32) + ry[h, 1].astype(F32))
            py[h, k:, :] = own[k:] + (ry[h, 0].astype(F32) + ry[h, 3].astype(F32))
            zs[h] = py[h, pl.ds(pl.multiple_of((1 - zh) * k, k), k), :].astype(BF)
            remote(zs.at[h], rz.at[h], rz_s.at[j], rz_r.at[j], tok=zpeer).start()
            track("rz", j, zs.at[h], rz.at[h], rz_s, rz_r)

    def piece(gg, h, j, n, e):
        k = n // 2
        return gg.at[h, c, pl.ds(pl.multiple_of(lax.rem(y + j, 4) * n + e * k, k), k)]

    def gather(h):
        for i, (gs, ra, rb, ry, py, zs, rz, gg, n) in enumerate(mats):
            j, k = 2 * h + i, n // 2
            done("rz", j)
            total = py[h, pl.ds(pl.multiple_of(zh * k, k), k), :] + rz[h].astype(F32)
            view = piece(gg, h, 0, n, zh)
            view[...] = total.astype(BF)
            remote(view, view, az_s.at[j], az_r.at[j], tok=zpeer).start()
            remote(view, view, ay_s.at[j], au_r.at[j], tok=up).start()
            remote(view, view, ay_s.at[j], ay_r.at[j], tok=down).start()
            track("az", j, view, piece(gg, h, 0, n, 1 - zh), az_s, az_r)

    def pass_on(h):
        for i, (gs, ra, rb, ry, py, zs, rz, gg, n) in enumerate(mats):
            j = 2 * h + i
            done("az", j)
            view = piece(gg, h, 0, n, 1 - zh)
            remote(view, view, ay_s.at[j], ad_r.at[j], tok=down).start()
            remote(view, view, ay_s.at[j], ay_r.at[j], tok=up).start()

    def relay_gather(h):
        for i, (gs, ra, rb, ry, py, zs, rz, gg, n) in enumerate(mats):
            j = 2 * h + i
            for sem, near, e, to in ((au_r, 3, zh, up), (ad_r, 1, 1 - zh, down)):
                view = piece(gg, h, near, n, e)
                pltpu.make_async_copy(view, view, sem.at[j]).wait()
                remote(view, view, ay_s.at[j], ay_r.at[j], tok=to).start()
            three = gg.at[h, c, pl.ds(0, 3 * n)]
            track("ay", j, three, gg.at[h, c, pl.ds(0, 2 * n)], ay_s, ay_r)

    def share(h):
        done("ay", 2 * h)
        mine = gg13.at[h, c, :, pl.ds(pl.multiple_of((1 - c) * HALF, HALF), HALF)]
        theirs = gg13.at[h, 1 - c, :, half]
        remote(mine, mine, fg_s.at[2 * h], fg_r.at[2 * h], tok=sib).start()
        track("fg", 2 * h, mine, theirs, fg_s, fg_r)
        done("ay", 2 * h + 1)
        remote(gg2.at[h, c], gg2.at[h, c], fg_s.at[2 * h + 1], fg_r.at[2 * h + 1], tok=sib).start()
        track("fg", 2 * h + 1, gg2.at[h, c], gg2.at[h, 1 - c], fg_s, fg_r)

    outs = (out1, out3, out2)

    def newton(parts):
        squares = jnp.sum(parts[0] ** 2) + jnp.sum(parts[1] ** 2)
        scale = 1.0 / (jnp.sqrt(jnp.full((8, 128), squares, F32)) + 1e-06)
        scale = scale[:1, :1]
        for part in range(2):
            piece_ = parts[part] * scale
            where = pl.ds(part * HALF, HALF)
            if parts[part].shape[0] == HALF:
                xs[where, :] = piece_
                xb[0, where, :] = piece_.astype(BF)
            else:
                xs[:, where] = piece_
                xb[0, :, where] = piece_.astype(BF)
        for step in range(ITERS):
            now, later = step % 2, (step + 1) % 2
            square = lax.dot_general(xb[now], xb[now], NT, preferred_element_type=F32)
            cube = jnp.dot(square.astype(BF), xb[now], preferred_element_type=F32)
            fresh = 1.5 * xs[...] - 0.5 * cube
            if step < ITERS - 1:
                xs[...] = fresh
                xb[later] = fresh.astype(BF)
        return fresh

    def renew(h, m, ortho):
        update = wv[m, h] - ortho
        new_norm = jnp.sqrt(jnp.sum(update * update, axis=0, keepdims=True) + 1e-06)
        fresh = update * (oldn[h, m, :1, :] / new_norm)
        nf[h, m] = fresh
        nb[m] = fresh.astype(BF)

    def newton_own(h):
        done("fg", 2 * h)
        xf[h, c] = newton([gg13[h, part, :, half].astype(F32) for part in range(2)]).astype(BF)
        remote(xf.at[h, c], xf.at[h, c], xf_s.at[h], xf_r.at[h], tok=sib).start()
        track("xf", h, xf.at[h, c], xf.at[h, 1 - c], xf_s, xf_r)

    def newton_second(h):
        done("fg", 2 * h + 1)
        renew(h, 2, newton([gg2[h, part].astype(F32) for part in range(2)]))

    def renew_both(h):
        renew(h, c, xf[h, c].astype(F32))
        done("xf", h)
        renew(h, 1 - c, xf[h, 1 - c].astype(F32))
        for m in range(3):
            sem = nf_sem.at[3 * h + m]
            pltpu.make_async_copy(nf.at[h, m], outs[m].at[h], sem).start()
            pending["nf_s", 3 * h + m] = (nf.at[h, m], sem)

    def apply(h):
        done("a2a", 4 + h)

        for tile in range(SPAN // TILE):
            at = pl.ds(tile * TILE, TILE)
            q = qin[h, at, :]
            y1 = jnp.dot(q, nb[0], preferred_element_type=F32)
            y3 = jnp.dot(q, nb[1], preferred_element_type=F32)
            qh[...] = (y1 * (1.0 / (1.0 + jnp.exp(-y1))) * y3).astype(BF)
            ov[h, at, :] = jnp.dot(qh[...], nb[2], preferred_element_type=F32).astype(BF)
            for i in range(tile * TILE // ROWS, (tile + 1) * TILE // ROWS):
                land = mixed.at[:, columns(hi, h)]
                if i == OWN:
                    pltpu.make_async_copy(ov.at[h, slot(i)], land, o_r.at[h]).start()
                else:
                    remote(ov.at[h, slot(i)], land, o_s.at[h], o_r.at[h], head=peers[i]).start()
        track("out", h, ov.at[h, pl.ds(0, SPAN - ROWS)], ov.at[h], o_s, o_r)

    def arrived(name, h):
        done(name, 2 * h)
        done(name, 2 * h + 1)

    steps = [
        lambda: forward(0),
        lambda: hidden_grads(0, c),
        lambda: arrived("fw", 0),
        lambda: hidden_grads(0, 1 - c),
        lambda: weight_grads(0),
        lambda: relay_y(0),
        lambda: forward(1),
        lambda: hidden_grads(1, c),
        lambda: arrived("fw", 1),
        lambda: hidden_grads(1, 1 - c),
        lambda: weight_grads(1),
        lambda: reduce_y(0),
        lambda: relay_y(1),
        lambda: [scatter(q_hbm, qin.at[h], 4 + h, h) for h in range(2)],
        lambda: [gather(0), pass_on(0), relay_gather(0)],
        lambda: reduce_y(1),
        lambda: [share(0), gather(1), newton_own(0), pass_on(1), relay_gather(1)],
        lambda: newton_second(0),
        lambda: renew_both(0),
        lambda: share(1),
        lambda: apply(0),
        lambda: newton_own(1),
        lambda: newton_second(1),
        lambda: renew_both(1),
        lambda: apply(1),
    ]
    for step in steps:
        step()

    for key in sorted(pending, key=lambda key: (key[0].endswith("_s"), key)):
        done(*key)


def hand_out(*refs):
    ins, outs, held, in_sem, out_sem = refs[:4], refs[4:8], refs[8:12], refs[12], refs[13]
    parts = [(0, None)] + [(i, h) for h in range(2) for i in (1, 2, 3)]

    def view(ref, h):
        return ref if h is None else ref.at[h]

    loads = [
        pltpu.make_async_copy(view(ins[i], h), view(held[i], h), in_sem.at[n]) for n, (i, h) in enumerate(parts)
    ]
    stores = [
        pltpu.make_async_copy(view(held[i], h), view(outs[i], h), out_sem.at[n]) for n, (i, h) in enumerate(parts)
    ]
    for load in loads:
        load.start()
    for load, store in zip(loads, stores):
        load.wait()
        store.start()
    for store in stores:
        store.wait()


def on_device(queries, keys, values, rates, w_first, w_gate, w_second):
    any_spec = pl.BlockSpec(memory_space=pl.ANY)
    dma = pltpu.SemaphoreType.DMA
    weights = jax.ShapeDtypeStruct(w_first.shape, F32)
    vm = pltpu.VMEM
    results = pl.pallas_call(
        kernel,
        out_shape=(jax.ShapeDtypeStruct(queries.shape, BF), weights, weights, weights),
        in_specs=[any_spec] * 7,
        out_specs=[any_spec] * 4,
        scratch_shapes=[
            vm((3, 2, DH, DH), F32),
            vm(values.shape, BF),
            vm(rates.shape[::-1], BF),
            vm(values.shape, BF),
            vm((2, 2, SPAN, DH), BF),
            vm((2, 2, SPAN, DH), BF),
            vm((2, SPAN, DH), BF),
            vm((2, DH, DH), BF),
            vm((2, HALF, DH), BF),
            vm((2, 3, 8, DH), F32),
            vm((2, SPAN, DH), BF),
            vm((2, SPAN, HALF), BF),
            vm((2, DH, DH), BF),
            vm((2, HALF, DH), BF),
            vm((2, 2, 64, DH), BF),
            vm((2, 2, 32, DH), BF),
            vm((2, 2, 64, DH), BF),
            vm((2, 2, 32, DH), BF),
            vm((2, 4, 64, DH), BF),
            vm((2, 4, 32, DH), BF),
            vm((2, 128, DH), F32),
            vm((2, 64, DH), F32),
            vm((2, 64, DH), BF),
            vm((2, 32, DH), BF),
            vm((2, 64, DH), BF),
            vm((2, 32, DH), BF),
            vm((2, 2, DH, DH), BF),
            vm((2, 2, HALF, DH), BF),
            vm((DH, DH), F32),
            vm((2, DH, DH), BF),
            vm((2, 2, DH, DH), BF),
            vm((3, DH, DH), BF),
            vm((TILE, DH), BF),
            vm((2, SPAN, DH), BF),
            vm((2, 3, DH, DH), F32),
            dma((5,)), dma((6,)), dma((6,)), dma((4,)), dma((4,)), dma((4,)), dma((4,)), dma((4,)),
            dma((4,)), dma((4,)), dma((4,)), dma((4,)), dma((4,)), dma((4,)), dma((4,)), dma((4,)),
            dma((4,)), dma((4,)), dma((2,)), dma((2,)), dma((2,)), dma((2,)), dma((6,)),
        ],
        compiler_params=pltpu.CompilerParams(
            collective_id=0, has_side_effects=True, vmem_limit_bytes=VMEM_BYTES
        ),
        name="layer",
    )(queries, keys, values, rates.T, w_first, w_gate, w_second)
    return pl.pallas_call(
        hand_out,
        out_shape=(jax.ShapeDtypeStruct(queries.shape, BF), weights, weights, weights),
        in_specs=[any_spec] * 4,
        out_specs=[any_spec] * 4,
        scratch_shapes=[vm(queries.shape, BF)] + [vm(w_first.shape, F32)] * 3 + [dma((7,)), dma((7,))],
        compiler_params=pltpu.CompilerParams(vmem_limit_bytes=VMEM_BYTES),
        name="hand_out",
    )(*results)


def solution(mesh):
    placed = (
        P(("head", "tok"), None),
        P(("head", "tok"), None),
        P(("head", "tok"), None),
        P(("head", "tok"), None),
        P("head", None, None),
        P("head", None, None),
        P("head", None, None),
    )
    return jax.shard_map(
        on_device,
        mesh=mesh,
        in_specs=placed,
        out_specs=(
            P(("head", "tok"), None),
            P("head", None, None),
            P("head", None, None),
            P("head", None, None),
        ),
        check_vma=False,
    )
```

```python
import functools

import jax
import jax.numpy as jnp
from jax import lax
from jax.experimental import pallas as pl
from jax.experimental.pallas import tpu as pltpu
from jax.sharding import PartitionSpec as P

ITERS = 3
BF = jnp.bfloat16
F32 = jnp.float32
MESH = pl.DeviceIdType.MESH
GROUPS = 8
ROWS = 64
DH = 512
HALF = 256
VMEM_BYTES = 56 * 1024 * 1024
SPAN = GROUPS * ROWS
TILE = 256
NT = (((1,), (1,)), ((), ()))
TN = (((0,), (0,)), ((), ()))
OFFSETS = ((2, 1), (2, 0), (1, 1), (3, 1), (1, 0), (3, 0), (0, 1))
BACK = tuple(OFFSETS.index(((4 - dx) % 4, dz)) for dx, dz in OFFSETS)
OWN = len(OFFSETS)


def kernel(
    q_hbm, k_hbm, v_hbm, r_hbm, w1_hbm, w3_hbm, w2_hbm,
    mixed, out1, out3, out2,
    wv, vv, rv, dv, kin, din, qin, wb13, wb2, oldn, dz, hid,
    gs13, gs2, ra13, ra2, rb13, rb2, ry13, ry2, py13, py2, zs13, zs2, rz13, rz2, gg13, gg2,
    xs, xb, xf, nb, qh, ov, nf,
    load_sem, a2a_s, a2a_r, fw_s, fw_r, ra_r, ry_s, ry_r, rz_s, rz_r,
    az_s, az_r, ay_s, ay_r, au_r, ad_r, fg_s, fg_r, xf_s, xf_r, o_s, o_r, nf_sem,
):
    hi = lax.axis_index("head")
    tk = lax.axis_index("tok")
    x, zl = hi // 2, lax.rem(hi, 2)
    zh, y, c = tk // 8, lax.rem(tk // 2, 4), lax.rem(tk, 2)
    peers = [lax.rem(x + dx, 4) * 2 + lax.rem(zl + dz_, 2) for dx, dz_ in OFFSETS]
    up, down = [zh * 8 + lax.rem(y + o, 4) * 2 + c for o in (1, 3)]
    zpeer = (1 - zh) * 8 + y * 2 + c
    sib = zh * 8 + y * 2 + (1 - c)

    def remote(src, dst, s, r, **where):
        return pltpu.make_async_remote_copy(
            src_ref=src, dst_ref=dst, send_sem=s, recv_sem=r, device_id=where, device_id_type=MESH
        )

    pending = {}

    def done(name, i):
        ref, sem = pending.pop((name, i))
        pltpu.make_async_copy(ref, ref, sem).wait()

    def track(name, i, sent, arriving, send_sems, recv_sems):
        pending[name + "_s", i] = (sent, send_sems.at[i])
        pending[name, i] = (arriving, recv_sems.at[i])

    barrier = pltpu.get_barrier_semaphore()
    for p in peers:
        pl.semaphore_signal(barrier, inc=1, device_id={"head": p}, device_id_type=MESH)
    for p in (up, down, zpeer, sib):
        pl.semaphore_signal(barrier, inc=1, device_id={"tok": p}, device_id_type=MESH)

    loads = [pltpu.make_async_copy(v_hbm, vv, load_sem.at[0]), pltpu.make_async_copy(r_hbm, rv, load_sem.at[1])]
    loads += [
        pltpu.make_async_copy(w, wv.at[m], load_sem.at[2 + m]) for m, w in enumerate((w1_hbm, w3_hbm, w2_hbm))
    ]
    for copy in loads:
        copy.start()

    pl.semaphore_wait(barrier, len(peers) + 4)

    def slot(i):
        return pl.ds(i * ROWS, ROWS)

    def columns(p, h):
        return pl.ds(pl.multiple_of((2 * p + h) * DH, DH), DH)

    def scatter(src, land, i, h):
        for p, b in zip(peers, BACK):
            remote(src.at[:, columns(p, h)], land.at[slot(b)], a2a_s.at[i], a2a_r.at[i], head=p).start()
        pltpu.make_async_copy(src.at[:, columns(hi, h)], land.at[slot(OWN)], a2a_r.at[i]).start()
        track("a2a", i, land.at[pl.ds(0, SPAN - ROWS)], land, a2a_s, a2a_r)

    def rate_values(h):
        rates = rv[...].astype(F32).T
        for g in range(h, 2 * GROUPS, 2):
            cols = slice(g * DH, (g + 1) * DH)
            dv[:, cols] = (-(rates[:, g : g + 1] * vv[:, cols].astype(F32))).astype(BF)

    scatter(k_hbm, kin.at[0, c], 0, 0)
    loads[0].wait()
    loads[1].wait()
    rate_values(0)
    scatter(dv, din.at[0, c], 1, 0)
    scatter(k_hbm, kin.at[1, c], 2, 1)
    rate_values(1)
    scatter(dv, din.at[1, c], 3, 1)

    for copy in loads[2:]:
        copy.wait()
    half = pl.ds(pl.multiple_of(c * HALF, HALF), HALF)
    for h in range(2):
        wb13[h, :, :HALF] = wv[0, h, :, half].astype(BF)
        wb13[h, :, HALF:] = wv[1, h, :, half].astype(BF)
        wb2[h] = wv[2, h, half, :].astype(BF)
        for m in range(3):
            w = wv[m, h]
            oldn[h, m] = jnp.broadcast_to(
                jnp.sqrt(jnp.sum(w * w, axis=0, keepdims=True) + 1e-06), (8, DH)
            )

    def forward(h):
        for i, buf in enumerate((kin, din)):
            j = 2 * h + i
            done("a2a", j)
            remote(buf.at[h, c], buf.at[h, c], fw_s.at[j], fw_r.at[j], tok=sib).start()
            track("fw", j, buf.at[h, c], buf.at[h, 1 - c], fw_s, fw_r)

    def hidden_grads(h, core):
        @pl.loop(0, SPAN // TILE)
        def _(step):
            at = pl.ds(pl.multiple_of(step * TILE, TILE), TILE)
            z = jnp.dot(kin[h, core, at, :], wb13[h], preferred_element_type=F32)
            dh = lax.dot_general(din[h, core, at, :], wb2[h], NT, preferred_element_type=F32)
            z1, z3 = z[:, :HALF], z[:, HALF:]
            sg = 1.0 / (1.0 + jnp.exp(-z1))
            act = z1 * sg
            hid[core, at, :] = (act * z3).astype(BF)
            dz[core, at, :HALF] = (dh * z3 * sg * (1.0 + z1 * (1.0 - sg))).astype(BF)
            dz[core, at, HALF:] = (dh * act).astype(BF)

    def block(j, rows, start=0, count=None):
        return pl.ds(pl.multiple_of(lax.rem(y + j, 4) * rows + start, 16), count or rows)

    def send_y(gs, ra, ry, n, i):
        k = n // 2
        remote(gs.at[block(2, n, 0, k)], ra.at[0], ry_s.at[i], ra_r.at[i], tok=up).start()
        remote(gs.at[block(2, n, k, k)], ra.at[1], ry_s.at[i], ra_r.at[i], tok=down).start()
        remote(gs.at[block(1, n, k, k)], ry.at[0], ry_s.at[i], ry_r.at[i], tok=up).start()
        remote(gs.at[block(3, n, 0, k)], ry.at[1], ry_s.at[i], ry_r.at[i], tok=down).start()
        pending["ra", i] = (ra, ra_r.at[i])

    def weight_grads(h):
        g = lax.dot_general(kin[h, 0], dz[0], TN, preferred_element_type=F32)
        g += lax.dot_general(kin[h, 1], dz[1], TN, preferred_element_type=F32)
        gs13[h] = g.astype(BF)
        send_y(gs13.at[h], ra13.at[h], ry13.at[h], 128, 2 * h)
        g = lax.dot_general(hid[0], din[h, 0], TN, preferred_element_type=F32)
        g += lax.dot_general(hid[1], din[h, 1], TN, preferred_element_type=F32)
        gs2[h] = g.astype(BF)
        send_y(gs2.at[h], ra2.at[h], ry2.at[h], 64, 2 * h + 1)

    mats = (
        (gs13, ra13, rb13, ry13, py13, zs13, rz13, gg13, 128),
        (gs2, ra2, rb2, ry2, py2, zs2, rz2, gg2, 64),
    )

    def relay_y(h):
        for i, (gs, ra, rb, ry, py, zs, rz, gg, n) in enumerate(mats):
            j, k = 2 * h + i, n // 2
            done("ra", j)
            rb[h, 0] = (gs[h, block(1, n, 0, k), :].astype(F32) + ra[h, 0].astype(F32)).astype(BF)
            rb[h, 1] = (gs[h, block(3, n, k, k), :].astype(F32) + ra[h, 1].astype(F32)).astype(BF)
            remote(rb.at[h, 0], ry.at[h, 2], ry_s.at[j], ry_r.at[j], tok=up).start()
            remote(rb.at[h, 1], ry.at[h, 3], ry_s.at[j], ry_r.at[j], tok=down).start()
            track("ry", j, gs.at[h, pl.ds(0, 3 * n)], ry.at[h], ry_s, ry_r)

    def reduce_y(h):
        for i, (gs, ra, rb, ry, py, zs, rz, gg, n) in enumerate(mats):
            j, k = 2 * h + i, n // 2
            done("ry", j)
            own = gs[h, block(0, n), :].astype(F32)
            py[h, :k, :] = own[:k] + (ry[h, 2].astype(F32) + ry[h, 1].astype(F32))
            py[h, k:, :] = own[k:] + (ry[h, 0].astype(F32) + ry[h, 3].astype(F32))
            zs[h] = py[h, pl.ds(pl.multiple_of((1 - zh) * k, k), k), :].astype(BF)
            remote(zs.at[h], rz.at[h], rz_s.at[j], rz_r.at[j], tok=zpeer).start()
            track("rz", j, zs.at[h], rz.at[h], rz_s, rz_r)

    def piece(gg, h, j, n, e):
        k = n // 2
        return gg.at[h, c, pl.ds(pl.multiple_of(lax.rem(y + j, 4) * n + e * k, k), k)]

    def gather(h):
        for i, (gs, ra, rb, ry, py, zs, rz, gg, n) in enumerate(mats):
            j, k = 2 * h + i, n // 2
            done("rz", j)
            total = py[h, pl.ds(pl.multiple_of(zh * k, k), k), :] + rz[h].astype(F32)
            view = piece(gg, h, 0, n, zh)
            view[...] = total.astype(BF)
            remote(view, view, az_s.at[j], az_r.at[j], tok=zpeer).start()
            remote(view, view, ay_s.at[j], au_r.at[j], tok=up).start()
            remote(view, view, ay_s.at[j], ay_r.at[j], tok=down).start()
            track("az", j, view, piece(gg, h, 0, n, 1 - zh), az_s, az_r)

    def pass_on(h):
        for i, (gs, ra, rb, ry, py, zs, rz, gg, n) in enumerate(mats):
            j = 2 * h + i
            done("az", j)
            view = piece(gg, h, 0, n, 1 - zh)
            remote(view, view, ay_s.at[j], ad_r.at[j], tok=down).start()
            remote(view, view, ay_s.at[j], ay_r.at[j], tok=up).start()

    def relay_gather(h):
        for i, (gs, ra, rb, ry, py, zs, rz, gg, n) in enumerate(mats):
            j = 2 * h + i
            for sem, near, e, to in ((au_r, 3, zh, up), (ad_r, 1, 1 - zh, down)):
                view = piece(gg, h, near, n, e)
                pltpu.make_async_copy(view, view, sem.at[j]).wait()
                remote(view, view, ay_s.at[j], ay_r.at[j], tok=to).start()
            three = gg.at[h, c, pl.ds(0, 3 * n)]
            track("ay", j, three, gg.at[h, c, pl.ds(0, 2 * n)], ay_s, ay_r)

    def share(h):
        done("ay", 2 * h)
        mine = gg13.at[h, c, :, pl.ds(pl.multiple_of((1 - c) * HALF, HALF), HALF)]
        theirs = gg13.at[h, 1 - c, :, half]
        remote(mine, mine, fg_s.at[2 * h], fg_r.at[2 * h], tok=sib).start()
        track("fg", 2 * h, mine, theirs, fg_s, fg_r)
        done("ay", 2 * h + 1)
        remote(gg2.at[h, c], gg2.at[h, c], fg_s.at[2 * h + 1], fg_r.at[2 * h + 1], tok=sib).start()
        track("fg", 2 * h + 1, gg2.at[h, c], gg2.at[h, 1 - c], fg_s, fg_r)

    outs = (out1, out3, out2)

    def newton(parts):
        squares = jnp.sum(parts[0] ** 2) + jnp.sum(parts[1] ** 2)
        scale = 1.0 / (jnp.sqrt(jnp.full((8, 128), squares, F32)) + 1e-06)
        scale = scale[:1, :1]
        for part in range(2):
            piece_ = parts[part] * scale
            where = pl.ds(part * HALF, HALF)
            if parts[part].shape[0] == HALF:
                xs[where, :] = piece_
                xb[0, where, :] = piece_.astype(BF)
            else:
                xs[:, where] = piece_
                xb[0, :, where] = piece_.astype(BF)
        for step in range(ITERS):
            now, later = step % 2, (step + 1) % 2
            square = lax.dot_general(xb[now], xb[now], NT, preferred_element_type=F32)
            cube = jnp.dot(square.astype(BF), xb[now], preferred_element_type=F32)
            fresh = 1.5 * xs[...] - 0.5 * cube
            if step < ITERS - 1:
                xs[...] = fresh
                xb[later] = fresh.astype(BF)
        return fresh

    def renew(h, m, ortho):
        update = wv[m, h] - ortho
        new_norm = jnp.sqrt(jnp.sum(update * update, axis=0, keepdims=True) + 1e-06)
        fresh = update * (oldn[h, m, :1, :] / new_norm)
        nf[h, m] = fresh
        nb[m] = fresh.astype(BF)

    def newton_own(h):
        done("fg", 2 * h)
        xf[h, c] = newton([gg13[h, part, :, half].astype(F32) for part in range(2)]).astype(BF)
        remote(xf.at[h, c], xf.at[h, c], xf_s.at[h], xf_r.at[h], tok=sib).start()
        track("xf", h, xf.at[h, c], xf.at[h, 1 - c], xf_s, xf_r)

    def newton_second(h):
        done("fg", 2 * h + 1)
        renew(h, 2, newton([gg2[h, part].astype(F32) for part in range(2)]))

    def renew_both(h):
        renew(h, c, xf[h, c].astype(F32))
        done("xf", h)
        renew(h, 1 - c, xf[h, 1 - c].astype(F32))
        for m in range(3):
            sem = nf_sem.at[3 * h + m]
            pltpu.make_async_copy(nf.at[h, m], outs[m].at[h], sem).start()
            pending["nf_s", 3 * h + m] = (nf.at[h, m], sem)

    def apply(h):
        done("a2a", 4 + h)

        for tile in range(SPAN // TILE):
            at = pl.ds(tile * TILE, TILE)
            q = qin[h, at, :]
            y1 = jnp.dot(q, nb[0], preferred_element_type=F32)
            y3 = jnp.dot(q, nb[1], preferred_element_type=F32)
            qh[...] = (y1 * (1.0 / (1.0 + jnp.exp(-y1))) * y3).astype(BF)
            ov[h, at, :] = jnp.dot(qh[...], nb[2], preferred_element_type=F32).astype(BF)
            for i in range(tile * TILE // ROWS, (tile + 1) * TILE // ROWS):
                land = mixed.at[:, columns(hi, h)]
                if i == OWN:
                    pltpu.make_async_copy(ov.at[h, slot(i)], land, o_r.at[h]).start()
                else:
                    remote(ov.at[h, slot(i)], land, o_s.at[h], o_r.at[h], head=peers[i]).start()
        track("out", h, ov.at[h, pl.ds(0, SPAN - ROWS)], ov.at[h], o_s, o_r)

    def arrived(name, h):
        done(name, 2 * h)
        done(name, 2 * h + 1)

    steps = [
        lambda: forward(0),
        lambda: hidden_grads(0, c),
        lambda: arrived("fw", 0),
        lambda: hidden_grads(0, 1 - c),
        lambda: weight_grads(0),
        lambda: relay_y(0),
        lambda: forward(1),
        lambda: scatter(q_hbm, qin.at[0], 4 + 0, 0),
        lambda: hidden_grads(1, c),
        lambda: reduce_y(0),
        lambda: arrived("fw", 1),
        lambda: hidden_grads(1, 1 - c),
        lambda: weight_grads(1),
        lambda: gather(0),
        lambda: relay_y(1),
        lambda: reduce_y(1),
        lambda: pass_on(0),
        lambda: relay_gather(0),
        lambda: gather(1),
        lambda: pass_on(1),
        lambda: share(0),
        lambda: relay_gather(1),
        lambda: newton_own(0),
        lambda: share(1),
        lambda: scatter(q_hbm, qin.at[1], 4 + 1, 1),
        lambda: newton_second(0),
        lambda: renew_both(0),
        lambda: apply(0),
        lambda: newton_own(1),
        lambda: newton_second(1),
        lambda: renew_both(1),
        lambda: apply(1),
    ]
    for step in steps:
        step()

    for key in sorted(pending, key=lambda key: (key[0].endswith("_s"), key)):
        done(*key)


def hand_out(*refs):
    ins, outs, held, in_sem, out_sem = refs[:4], refs[4:8], refs[8:12], refs[12], refs[13]
    parts = [(i, 0, row) for i in (1, 2, 3) for row in (0, HALF)]
    parts += [(0, 0, 0)] + [(i, 1, row) for i in (1, 2, 3) for row in (0, HALF)]

    def view(i, ref, h, row):
        return ref.at[h, pl.ds(row, HALF)] if i else ref

    loads = [
        pltpu.make_async_copy(view(i, ins[i], h, r), view(i, held[i], h, r), in_sem.at[n])
        for n, (i, h, r) in enumerate(parts)
    ]
    stores = [
        pltpu.make_async_copy(view(i, held[i], h, r), view(i, outs[i], h, r), out_sem.at[n])
        for n, (i, h, r) in enumerate(parts)
    ]
    for load in loads:
        load.start()
    for load, store in zip(loads, stores):
        load.wait()
        store.start()
    for store in stores:
        store.wait()


def on_device(queries, keys, values, rates, w_first, w_gate, w_second):
    any_spec = pl.BlockSpec(memory_space=pl.ANY)
    dma = pltpu.SemaphoreType.DMA
    weights = jax.ShapeDtypeStruct(w_first.shape, F32)
    vm = pltpu.VMEM
    results = pl.pallas_call(
        kernel,
        out_shape=(jax.ShapeDtypeStruct(queries.shape, BF), weights, weights, weights),
        in_specs=[any_spec] * 7,
        out_specs=[any_spec] * 4,
        scratch_shapes=[
            vm((3, 2, DH, DH), F32),
            vm(values.shape, BF),
            vm(rates.shape[::-1], BF),
            vm(values.shape, BF),
            vm((2, 2, SPAN, DH), BF),
            vm((2, 2, SPAN, DH), BF),
            vm((2, SPAN, DH), BF),
            vm((2, DH, DH), BF),
            vm((2, HALF, DH), BF),
            vm((2, 3, 8, DH), F32),
            vm((2, SPAN, DH), BF),
            vm((2, SPAN, HALF), BF),
            vm((2, DH, DH), BF),
            vm((2, HALF, DH), BF),
            vm((2, 2, 64, DH), BF),
            vm((2, 2, 32, DH), BF),
            vm((2, 2, 64, DH), BF),
            vm((2, 2, 32, DH), BF),
            vm((2, 4, 64, DH), BF),
            vm((2, 4, 32, DH), BF),
            vm((2, 128, DH), F32),
            vm((2, 64, DH), F32),
            vm((2, 64, DH), BF),
            vm((2, 32, DH), BF),
            vm((2, 64, DH), BF),
            vm((2, 32, DH), BF),
            vm((2, 2, DH, DH), BF),
            vm((2, 2, HALF, DH), BF),
            vm((DH, DH), F32),
            vm((2, DH, DH), BF),
            vm((2, 2, DH, DH), BF),
            vm((3, DH, DH), BF),
            vm((TILE, DH), BF),
            vm((2, SPAN, DH), BF),
            vm((2, 3, DH, DH), F32),
            dma((5,)), dma((6,)), dma((6,)), dma((4,)), dma((4,)), dma((4,)), dma((4,)), dma((4,)),
            dma((4,)), dma((4,)), dma((4,)), dma((4,)), dma((4,)), dma((4,)), dma((4,)), dma((4,)),
            dma((4,)), dma((4,)), dma((2,)), dma((2,)), dma((2,)), dma((2,)), dma((6,)),
        ],
        compiler_params=pltpu.CompilerParams(
            collective_id=0, has_side_effects=True, vmem_limit_bytes=VMEM_BYTES
        ),
        name="layer",
    )(queries, keys, values, rates.T, w_first, w_gate, w_second)
    return pl.pallas_call(
        hand_out,
        out_shape=(jax.ShapeDtypeStruct(queries.shape, BF), weights, weights, weights),
        in_specs=[any_spec] * 4,
        out_specs=[any_spec] * 4,
        scratch_shapes=[vm(queries.shape, BF)] + [vm(w_first.shape, F32)] * 3 + [dma((13,)), dma((13,))],
        compiler_params=pltpu.CompilerParams(vmem_limit_bytes=VMEM_BYTES),
        name="hand_out",
    )(*results)


def solution(mesh):
    placed = (
        P(("head", "tok"), None),
        P(("head", "tok"), None),
        P(("head", "tok"), None),
        P(("head", "tok"), None),
        P("head", None, None),
        P("head", None, None),
        P("head", None, None),
    )
    return jax.shard_map(
        on_device,
        mesh=mesh,
        in_specs=placed,
        out_specs=(
            P(("head", "tok"), None),
            P("head", None, None),
            P("head", None, None),
            P("head", None, None),
        ),
        check_vma=False,
    )
```

```python
import functools

import jax
import jax.numpy as jnp
from jax import lax
from jax.experimental import pallas as pl
from jax.experimental.pallas import tpu as pltpu
from jax.sharding import PartitionSpec as P

ITERS = 3
BF = jnp.bfloat16
F32 = jnp.float32
MESH = pl.DeviceIdType.MESH
GROUPS = 8
ROWS = 64
DH = 512
HALF = 256
VMEM_BYTES = 56 * 1024 * 1024
SPAN = GROUPS * ROWS
TILE = 256
NT = (((1,), (1,)), ((), ()))
TN = (((0,), (0,)), ((), ()))
OFFSETS = ((1, 0), (3, 0), (0, 1), (2, 0), (1, 1), (3, 1), (2, 1))
BACK = tuple(OFFSETS.index(((4 - dx) % 4, dz)) for dx, dz in OFFSETS)
OWN = len(OFFSETS)


def kernel(
    q_hbm, k_hbm, v_hbm, r_hbm, w1_hbm, w3_hbm, w2_hbm,
    mixed, out1, out3, out2,
    wv, vv, rv, dv, kin, din, qin, wb13, wb2, oldn, dz, hid,
    gs13, gs2, ra13, ra2, rb13, rb2, ry13, ry2, py13, py2, zs13, zs2, rz13, rz2, gg13, gg2,
    xs, xb, xf, nb, qh, ov, nf,
    load_sem, a2a_s, a2a_r, fw_s, fw_r, ra_r, ry_s, ry_r, rz_s, rz_r,
    az_s, az_r, ay_s, ay_r, au_r, ad_r, fg_s, fg_r, xf_s, xf_r, o_s, o_r, nf_sem,
):
    hi = lax.axis_index("head")
    tk = lax.axis_index("tok")
    x, zl = hi // 2, lax.rem(hi, 2)
    zh, y, c = tk // 8, lax.rem(tk // 2, 4), lax.rem(tk, 2)
    peers = [lax.rem(x + dx, 4) * 2 + lax.rem(zl + dz_, 2) for dx, dz_ in OFFSETS]
    up, down = [zh * 8 + lax.rem(y + o, 4) * 2 + c for o in (1, 3)]
    zpeer = (1 - zh) * 8 + y * 2 + c
    sib = zh * 8 + y * 2 + (1 - c)

    def remote(src, dst, s, r, **where):
        return pltpu.make_async_remote_copy(
            src_ref=src, dst_ref=dst, send_sem=s, recv_sem=r, device_id=where, device_id_type=MESH
        )

    pending = {}

    def done(name, i):
        ref, sem = pending.pop((name, i))
        pltpu.make_async_copy(ref, ref, sem).wait()

    def track(name, i, sent, arriving, send_sems, recv_sems):
        pending[name + "_s", i] = (sent, send_sems.at[i])
        pending[name, i] = (arriving, recv_sems.at[i])

    barrier = pltpu.get_barrier_semaphore()
    for p in peers:
        pl.semaphore_signal(barrier, inc=1, device_id={"head": p}, device_id_type=MESH)
    for p in (up, down, zpeer, sib):
        pl.semaphore_signal(barrier, inc=1, device_id={"tok": p}, device_id_type=MESH)

    loads = [pltpu.make_async_copy(v_hbm, vv, load_sem.at[0]), pltpu.make_async_copy(r_hbm, rv, load_sem.at[1])]
    loads += [
        pltpu.make_async_copy(w, wv.at[m], load_sem.at[2 + m]) for m, w in enumerate((w1_hbm, w3_hbm, w2_hbm))
    ]
    for copy in loads:
        copy.start()

    pl.semaphore_wait(barrier, len(peers) + 4)

    def slot(i):
        return pl.ds(i * ROWS, ROWS)

    def columns(p, h):
        return pl.ds(pl.multiple_of((2 * p + h) * DH, DH), DH)

    def scatter(src, land, i, h):
        for p, b in zip(peers, BACK):
            remote(src.at[:, columns(p, h)], land.at[slot(b)], a2a_s.at[i], a2a_r.at[i], head=p).start()
        pltpu.make_async_copy(src.at[:, columns(hi, h)], land.at[slot(OWN)], a2a_r.at[i]).start()
        track("a2a", i, land.at[pl.ds(0, SPAN - ROWS)], land, a2a_s, a2a_r)

    def rate_values(h):
        rates = rv[...].astype(F32).T
        for g in range(h, 2 * GROUPS, 2):
            cols = slice(g * DH, (g + 1) * DH)
            dv[:, cols] = (-(rates[:, g : g + 1] * vv[:, cols].astype(F32))).astype(BF)

    scatter(k_hbm, kin.at[0, c], 0, 0)
    loads[0].wait()
    loads[1].wait()
    rate_values(0)
    scatter(dv, din.at[0, c], 1, 0)
    scatter(k_hbm, kin.at[1, c], 2, 1)
    rate_values(1)
    scatter(dv, din.at[1, c], 3, 1)

    for copy in loads[2:]:
        copy.wait()
    half = pl.ds(pl.multiple_of(c * HALF, HALF), HALF)
    for h in range(2):
        wb13[h, :, :HALF] = wv[0, h, :, half].astype(BF)
        wb13[h, :, HALF:] = wv[1, h, :, half].astype(BF)
        wb2[h] = wv[2, h, half, :].astype(BF)
        for m in range(3):
            w = wv[m, h]
            oldn[h, m] = jnp.broadcast_to(
                jnp.sqrt(jnp.sum(w * w, axis=0, keepdims=True) + 1e-06), (8, DH)
            )

    def forward(h):
        for i, buf in enumerate((kin, din)):
            j = 2 * h + i
            done("a2a", j)
            remote(buf.at[h, c], buf.at[h, c], fw_s.at[j], fw_r.at[j], tok=sib).start()
            track("fw", j, buf.at[h, c], buf.at[h, 1 - c], fw_s, fw_r)

    def hidden_grads(h, core):
        @pl.loop(0, SPAN // TILE)
        def _(step):
            at = pl.ds(pl.multiple_of(step * TILE, TILE), TILE)
            z = jnp.dot(kin[h, core, at, :], wb13[h], preferred_element_type=F32)
            dh = lax.dot_general(din[h, core, at, :], wb2[h], NT, preferred_element_type=F32)
            z1, z3 = z[:, :HALF], z[:, HALF:]
            sg = 1.0 / (1.0 + jnp.exp(-z1))
            act = z1 * sg
            hid[core, at, :] = (act * z3).astype(BF)
            dz[core, at, :HALF] = (dh * z3 * sg * (1.0 + z1 * (1.0 - sg))).astype(BF)
            dz[core, at, HALF:] = (dh * act).astype(BF)

    def block(j, rows, start=0, count=None):
        return pl.ds(pl.multiple_of(lax.rem(y + j, 4) * rows + start, 16), count or rows)

    def send_y(gs, ra, ry, n, i):
        k = n // 2
        remote(gs.at[block(2, n, 0, k)], ra.at[0], ry_s.at[i], ra_r.at[i], tok=up).start()
        remote(gs.at[block(2, n, k, k)], ra.at[1], ry_s.at[i], ra_r.at[i], tok=down).start()
        remote(gs.at[block(1, n, k, k)], ry.at[0], ry_s.at[i], ry_r.at[i], tok=up).start()
        remote(gs.at[block(3, n, 0, k)], ry.at[1], ry_s.at[i], ry_r.at[i], tok=down).start()
        pending["ra", i] = (ra, ra_r.at[i])

    def weight_grads(h):
        g = lax.dot_general(kin[h, 0], dz[0], TN, preferred_element_type=F32)
        g += lax.dot_general(kin[h, 1], dz[1], TN, preferred_element_type=F32)
        gs13[h] = g.astype(BF)
        send_y(gs13.at[h], ra13.at[h], ry13.at[h], 128, 2 * h)
        g = lax.dot_general(hid[0], din[h, 0], TN, preferred_element_type=F32)
        g += lax.dot_general(hid[1], din[h, 1], TN, preferred_element_type=F32)
        gs2[h] = g.astype(BF)
        send_y(gs2.at[h], ra2.at[h], ry2.at[h], 64, 2 * h + 1)

    mats = (
        (gs13, ra13, rb13, ry13, py13, zs13, rz13, gg13, 128),
        (gs2, ra2, rb2, ry2, py2, zs2, rz2, gg2, 64),
    )

    def relay_y(h):
        for i, (gs, ra, rb, ry, py, zs, rz, gg, n) in enumerate(mats):
            j, k = 2 * h + i, n // 2
            done("ra", j)
            rb[h, 0] = (gs[h, block(1, n, 0, k), :].astype(F32) + ra[h, 0].astype(F32)).astype(BF)
            rb[h, 1] = (gs[h, block(3, n, k, k), :].astype(F32) + ra[h, 1].astype(F32)).astype(BF)
            remote(rb.at[h, 0], ry.at[h, 2], ry_s.at[j], ry_r.at[j], tok=up).start()
            remote(rb.at[h, 1], ry.at[h, 3], ry_s.at[j], ry_r.at[j], tok=down).start()
            track("ry", j, gs.at[h, pl.ds(0, 3 * n)], ry.at[h], ry_s, ry_r)

    def reduce_y(h):
        for i, (gs, ra, rb, ry, py, zs, rz, gg, n) in enumerate(mats):
            j, k = 2 * h + i, n // 2
            done("ry", j)
            own = gs[h, block(0, n), :].astype(F32)
            py[h, :k, :] = own[:k] + (ry[h, 2].astype(F32) + ry[h, 1].astype(F32))
            py[h, k:, :] = own[k:] + (ry[h, 0].astype(F32) + ry[h, 3].astype(F32))
            zs[h] = py[h, pl.ds(pl.multiple_of((1 - zh) * k, k), k), :].astype(BF)
            remote(zs.at[h], rz.at[h], rz_s.at[j], rz_r.at[j], tok=zpeer).start()
            track("rz", j, zs.at[h], rz.at[h], rz_s, rz_r)

    def piece(gg, h, j, n, e):
        k = n // 2
        return gg.at[h, c, pl.ds(pl.multiple_of(lax.rem(y + j, 4) * n + e * k, k), k)]

    def gather(h):
        for i, (gs, ra, rb, ry, py, zs, rz, gg, n) in enumerate(mats):
            j, k = 2 * h + i, n // 2
            done("rz", j)
            total = py[h, pl.ds(pl.multiple_of(zh * k, k), k), :] + rz[h].astype(F32)
            view = piece(gg, h, 0, n, zh)
            view[...] = total.astype(BF)
            remote(view, view, az_s.at[j], az_r.at[j], tok=zpeer).start()
            remote(view, view, ay_s.at[j], au_r.at[j], tok=up).start()
            remote(view, view, ay_s.at[j], ay_r.at[j], tok=down).start()
            track("az", j, view, piece(gg, h, 0, n, 1 - zh), az_s, az_r)

    def pass_on(h):
        for i, (gs, ra, rb, ry, py, zs, rz, gg, n) in enumerate(mats):
            j = 2 * h + i
            done("az", j)
            view = piece(gg, h, 0, n, 1 - zh)
            remote(view, view, ay_s.at[j], ad_r.at[j], tok=down).start()
            remote(view, view, ay_s.at[j], ay_r.at[j], tok=up).start()

    def relay_gather(h):
        for i, (gs, ra, rb, ry, py, zs, rz, gg, n) in enumerate(mats):
            j = 2 * h + i
            for sem, near, e, to in ((au_r, 3, zh, up), (ad_r, 1, 1 - zh, down)):
                view = piece(gg, h, near, n, e)
                pltpu.make_async_copy(view, view, sem.at[j]).wait()
                remote(view, view, ay_s.at[j], ay_r.at[j], tok=to).start()
            three = gg.at[h, c, pl.ds(0, 3 * n)]
            track("ay", j, three, gg.at[h, c, pl.ds(0, 2 * n)], ay_s, ay_r)

    def share(h):
        done("ay", 2 * h)
        mine = gg13.at[h, c, :, pl.ds(pl.multiple_of((1 - c) * HALF, HALF), HALF)]
        theirs = gg13.at[h, 1 - c, :, half]
        remote(mine, mine, fg_s.at[2 * h], fg_r.at[2 * h], tok=sib).start()
        track("fg", 2 * h, mine, theirs, fg_s, fg_r)
        done("ay", 2 * h + 1)
        remote(gg2.at[h, c], gg2.at[h, c], fg_s.at[2 * h + 1], fg_r.at[2 * h + 1], tok=sib).start()
        track("fg", 2 * h + 1, gg2.at[h, c], gg2.at[h, 1 - c], fg_s, fg_r)

    outs = (out1, out3, out2)

    def newton(parts):
        squares = jnp.sum(parts[0] ** 2) + jnp.sum(parts[1] ** 2)
        scale = 1.0 / (jnp.sqrt(jnp.full((8, 128), squares, F32)) + 1e-06)
        scale = scale[:1, :1]
        for part in range(2):
            piece_ = parts[part] * scale
            where = pl.ds(part * HALF, HALF)
            if parts[part].shape[0] == HALF:
                xs[where, :] = piece_
                xb[0, where, :] = piece_.astype(BF)
            else:
                xs[:, where] = piece_
                xb[0, :, where] = piece_.astype(BF)
        for step in range(ITERS):
            now, later = step % 2, (step + 1) % 2
            square = lax.dot_general(xb[now], xb[now], NT, preferred_element_type=F32)
            cube = jnp.dot(square.astype(BF), xb[now], preferred_element_type=F32)
            fresh = 1.5 * xs[...] - 0.5 * cube
            if step < ITERS - 1:
                xs[...] = fresh
                xb[later] = fresh.astype(BF)
        return fresh

    def renew(h, m, ortho):
        update = wv[m, h] - ortho
        new_norm = jnp.sqrt(jnp.sum(update * update, axis=0, keepdims=True) + 1e-06)
        fresh = update * (oldn[h, m, :1, :] / new_norm)
        nf[h, m] = fresh
        nb[m] = fresh.astype(BF)

    def newton_own(h):
        done("fg", 2 * h)
        xf[h, c] = newton([gg13[h, part, :, half].astype(F32) for part in range(2)]).astype(BF)
        remote(xf.at[h, c], xf.at[h, c], xf_s.at[h], xf_r.at[h], tok=sib).start()
        track("xf", h, xf.at[h, c], xf.at[h, 1 - c], xf_s, xf_r)

    def newton_second(h):
        done("fg", 2 * h + 1)
        renew(h, 2, newton([gg2[h, part].astype(F32) for part in range(2)]))

    def renew_both(h):
        renew(h, c, xf[h, c].astype(F32))
        done("xf", h)
        renew(h, 1 - c, xf[h, 1 - c].astype(F32))
        for m in range(3):
            sem = nf_sem.at[3 * h + m]
            pltpu.make_async_copy(nf.at[h, m], outs[m].at[h], sem).start()
            pending["nf_s", 3 * h + m] = (nf.at[h, m], sem)

    def apply(h):
        done("a2a", 4 + h)

        for tile in range(SPAN // TILE):
            at = pl.ds(tile * TILE, TILE)
            q = qin[h, at, :]
            y1 = jnp.dot(q, nb[0], preferred_element_type=F32)
            y3 = jnp.dot(q, nb[1], preferred_element_type=F32)
            qh[...] = (y1 * (1.0 / (1.0 + jnp.exp(-y1))) * y3).astype(BF)
            ov[h, at, :] = jnp.dot(qh[...], nb[2], preferred_element_type=F32).astype(BF)
            for i in range(tile * TILE // ROWS, (tile + 1) * TILE // ROWS):
                land = mixed.at[:, columns(hi, h)]
                if i == OWN:
                    pltpu.make_async_copy(ov.at[h, slot(i)], land, o_r.at[h]).start()
                else:
                    remote(ov.at[h, slot(i)], land, o_s.at[h], o_r.at[h], head=peers[i]).start()
        track("out", h, ov.at[h, pl.ds(0, SPAN - ROWS)], ov.at[h], o_s, o_r)

    def arrived(name, h):
        done(name, 2 * h)
        done(name, 2 * h + 1)

    steps = [
        lambda: forward(0),
        lambda: hidden_grads(0, c),
        lambda: arrived("fw", 0),
        lambda: hidden_grads(0, 1 - c),
        lambda: weight_grads(0),
        lambda: relay_y(0),
        lambda: forward(1),
        lambda: scatter(q_hbm, qin.at[0], 4 + 0, 0),
        lambda: hidden_grads(1, c),
        lambda: reduce_y(0),
        lambda: arrived("fw", 1),
        lambda: hidden_grads(1, 1 - c),
        lambda: weight_grads(1),
        lambda: gather(0),
        lambda: relay_y(1),
        lambda: reduce_y(1),
        lambda: pass_on(0),
        lambda: relay_gather(0),
        lambda: gather(1),
        lambda: share(0),
        lambda: pass_on(1),
        lambda: newton_own(0),
        lambda: relay_gather(1),
        lambda: newton_second(0),
        lambda: share(1),
        lambda: scatter(q_hbm, qin.at[1], 4 + 1, 1),
        lambda: renew_both(0),
        lambda: apply(0),
        lambda: newton_own(1),
        lambda: newton_second(1),
        lambda: renew_both(1),
        lambda: apply(1),
    ]
    for step in steps:
        step()

    for key in sorted(pending, key=lambda key: (key[0].endswith("_s"), key)):
        done(*key)


def hand_out(*refs):
    ins, outs, held, in_sem, out_sem = refs[:4], refs[4:8], refs[8:12], refs[12], refs[13]
    parts = [(i, 0, row) for i in (1, 2, 3) for row in (0, HALF)]
    parts += [(0, 0, 0)] + [(i, 1, row) for i in (1, 2, 3) for row in (0, HALF)]

    def view(i, ref, h, row):
        return ref.at[h, pl.ds(row, HALF)] if i else ref

    loads = [
        pltpu.make_async_copy(view(i, ins[i], h, r), view(i, held[i], h, r), in_sem.at[n])
        for n, (i, h, r) in enumerate(parts)
    ]
    stores = [
        pltpu.make_async_copy(view(i, held[i], h, r), view(i, outs[i], h, r), out_sem.at[n])
        for n, (i, h, r) in enumerate(parts)
    ]
    for load in loads:
        load.start()
    for load, store in zip(loads, stores):
        load.wait()
        store.start()
    for store in stores:
        store.wait()


def on_device(queries, keys, values, rates, w_first, w_gate, w_second):
    any_spec = pl.BlockSpec(memory_space=pl.ANY)
    dma = pltpu.SemaphoreType.DMA
    weights = jax.ShapeDtypeStruct(w_first.shape, F32)
    vm = pltpu.VMEM
    results = pl.pallas_call(
        kernel,
        out_shape=(jax.ShapeDtypeStruct(queries.shape, BF), weights, weights, weights),
        in_specs=[any_spec] * 7,
        out_specs=[any_spec] * 4,
        scratch_shapes=[
            vm((3, 2, DH, DH), F32),
            vm(values.shape, BF),
            vm(rates.shape[::-1], BF),
            vm(values.shape, BF),
            vm((2, 2, SPAN, DH), BF),
            vm((2, 2, SPAN, DH), BF),
            vm((2, SPAN, DH), BF),
            vm((2, DH, DH), BF),
            vm((2, HALF, DH), BF),
            vm((2, 3, 8, DH), F32),
            vm((2, SPAN, DH), BF),
            vm((2, SPAN, HALF), BF),
            vm((2, DH, DH), BF),
            vm((2, HALF, DH), BF),
            vm((2, 2, 64, DH), BF),
            vm((2, 2, 32, DH), BF),
            vm((2, 2, 64, DH), BF),
            vm((2, 2, 32, DH), BF),
            vm((2, 4, 64, DH), BF),
            vm((2, 4, 32, DH), BF),
            vm((2, 128, DH), F32),
            vm((2, 64, DH), F32),
            vm((2, 64, DH), BF),
            vm((2, 32, DH), BF),
            vm((2, 64, DH), BF),
            vm((2, 32, DH), BF),
            vm((2, 2, DH, DH), BF),
            vm((2, 2, HALF, DH), BF),
            vm((DH, DH), F32),
            vm((2, DH, DH), BF),
            vm((2, 2, DH, DH), BF),
            vm((3, DH, DH), BF),
            vm((TILE, DH), BF),
            vm((2, SPAN, DH), BF),
            vm((2, 3, DH, DH), F32),
            dma((5,)), dma((6,)), dma((6,)), dma((4,)), dma((4,)), dma((4,)), dma((4,)), dma((4,)),
            dma((4,)), dma((4,)), dma((4,)), dma((4,)), dma((4,)), dma((4,)), dma((4,)), dma((4,)),
            dma((4,)), dma((4,)), dma((2,)), dma((2,)), dma((2,)), dma((2,)), dma((6,)),
        ],
        compiler_params=pltpu.CompilerParams(
            collective_id=0, has_side_effects=True, vmem_limit_bytes=VMEM_BYTES
        ),
        name="layer",
    )(queries, keys, values, rates.T, w_first, w_gate, w_second)
    return pl.pallas_call(
        hand_out,
        out_shape=(jax.ShapeDtypeStruct(queries.shape, BF), weights, weights, weights),
        in_specs=[any_spec] * 4,
        out_specs=[any_spec] * 4,
        scratch_shapes=[vm(queries.shape, BF)] + [vm(w_first.shape, F32)] * 3 + [dma((13,)), dma((13,))],
        compiler_params=pltpu.CompilerParams(vmem_limit_bytes=VMEM_BYTES),
        name="hand_out",
    )(*results)


def solution(mesh):
    placed = (
        P(("head", "tok"), None),
        P(("head", "tok"), None),
        P(("head", "tok"), None),
        P(("head", "tok"), None),
        P("head", None, None),
        P("head", None, None),
        P("head", None, None),
    )
    return jax.shard_map(
        on_device,
        mesh=mesh,
        in_specs=placed,
        out_specs=(
            P(("head", "tok"), None),
            P("head", None, None),
            P("head", None, None),
            P("head", None, None),
        ),
        check_vma=False,
    )
```

```python
import functools

import jax
import jax.numpy as jnp
from jax import lax
from jax.experimental import pallas as pl
from jax.experimental.pallas import tpu as pltpu
from jax.sharding import PartitionSpec as P

ITERS = 3
BF = jnp.bfloat16
F32 = jnp.float32
MESH = pl.DeviceIdType.MESH
GROUPS = 8
ROWS = 64
DH = 512
HALF = 256
VMEM_BYTES = 56 * 1024 * 1024
SPAN = GROUPS * ROWS
TILE = 256
NT = (((1,), (1,)), ((), ()))
TN = (((0,), (0,)), ((), ()))
OFFSETS = ((2, 1), (2, 0), (1, 1), (3, 1), (1, 0), (3, 0), (0, 1))
BACK = tuple(OFFSETS.index(((4 - dx) % 4, dz)) for dx, dz in OFFSETS)
OWN = len(OFFSETS)


def kernel(
    q_hbm, k_hbm, v_hbm, r_hbm, w1_hbm, w3_hbm, w2_hbm,
    mixed, out1, out3, out2,
    wv, vv, rv, dv, kin, din, qin, wb13, wb2, oldn, dz, hid,
    gs13, gs2, ra13, ra2, rb13, rb2, ry13, ry2, py13, py2, zs13, zs2, rz13, rz2, gg13, gg2,
    xs, xb, xf, nb, qh, ov, nf,
    load_sem, a2a_s, a2a_r, fw_s, fw_r, ra_r, ry_s, ry_r, rz_s, rz_r,
    az_s, az_r, ay_s, ay_r, au_r, ad_r, fg_s, fg_r, xf_s, xf_r, o_s, o_r, nf_sem,
):
    hi = lax.axis_index("head")
    tk = lax.axis_index("tok")
    x, zl = hi // 2, lax.rem(hi, 2)
    zh, y, c = tk // 8, lax.rem(tk // 2, 4), lax.rem(tk, 2)
    peers = [lax.rem(x + dx, 4) * 2 + lax.rem(zl + dz_, 2) for dx, dz_ in OFFSETS]
    up, down = [zh * 8 + lax.rem(y + o, 4) * 2 + c for o in (1, 3)]
    zpeer = (1 - zh) * 8 + y * 2 + c
    sib = zh * 8 + y * 2 + (1 - c)

    def remote(src, dst, s, r, **where):
        return pltpu.make_async_remote_copy(
            src_ref=src, dst_ref=dst, send_sem=s, recv_sem=r, device_id=where, device_id_type=MESH
        )

    pending = {}

    def done(name, i):
        ref, sem = pending.pop((name, i))
        pltpu.make_async_copy(ref, ref, sem).wait()

    def track(name, i, sent, arriving, send_sems, recv_sems):
        pending[name + "_s", i] = (sent, send_sems.at[i])
        pending[name, i] = (arriving, recv_sems.at[i])

    barrier = pltpu.get_barrier_semaphore()
    for p in peers:
        pl.semaphore_signal(barrier, inc=1, device_id={"head": p}, device_id_type=MESH)
    for p in (up, down, zpeer, sib):
        pl.semaphore_signal(barrier, inc=1, device_id={"tok": p}, device_id_type=MESH)

    loads = [pltpu.make_async_copy(v_hbm, vv, load_sem.at[0]), pltpu.make_async_copy(r_hbm, rv, load_sem.at[1])]
    loads += [
        pltpu.make_async_copy(w, wv.at[m], load_sem.at[2 + m]) for m, w in enumerate((w1_hbm, w3_hbm, w2_hbm))
    ]
    for copy in loads:
        copy.start()

    pl.semaphore_wait(barrier, len(peers) + 4)

    def slot(i):
        return pl.ds(i * ROWS, ROWS)

    def columns(p, h):
        return pl.ds(pl.multiple_of((2 * p + h) * DH, DH), DH)

    def scatter(src, land, i, h):
        for p, b in reversed(tuple(zip(peers, BACK))):
            remote(src.at[:, columns(p, h)], land.at[slot(b)], a2a_s.at[i], a2a_r.at[i], head=p).start()
        pltpu.make_async_copy(src.at[:, columns(hi, h)], land.at[slot(OWN)], a2a_r.at[i]).start()
        track("a2a", i, land.at[pl.ds(0, SPAN - ROWS)], land, a2a_s, a2a_r)

    def rate_values(h):
        rates = rv[...].astype(F32).T
        for g in range(h, 2 * GROUPS, 2):
            cols = slice(g * DH, (g + 1) * DH)
            dv[:, cols] = (-(rates[:, g : g + 1] * vv[:, cols].astype(F32))).astype(BF)

    scatter(k_hbm, kin.at[0, c], 0, 0)
    loads[0].wait()
    loads[1].wait()
    rate_values(0)
    scatter(dv, din.at[0, c], 1, 0)
    scatter(k_hbm, kin.at[1, c], 2, 1)
    rate_values(1)
    scatter(dv, din.at[1, c], 3, 1)

    for copy in loads[2:]:
        copy.wait()
    half = pl.ds(pl.multiple_of(c * HALF, HALF), HALF)
    for h in range(2):
        wb13[h, :, :HALF] = wv[0, h, :, half].astype(BF)
        wb13[h, :, HALF:] = wv[1, h, :, half].astype(BF)
        wb2[h] = wv[2, h, half, :].astype(BF)
        for m in range(3):
            w = wv[m, h]
            oldn[h, m] = jnp.broadcast_to(
                jnp.sqrt(jnp.sum(w * w, axis=0, keepdims=True) + 1e-06), (8, DH)
            )

    def forward(h):
        for i, buf in enumerate((kin, din)):
            j = 2 * h + i
            done("a2a", j)
            remote(buf.at[h, c], buf.at[h, c], fw_s.at[j], fw_r.at[j], tok=sib).start()
            track("fw", j, buf.at[h, c], buf.at[h, 1 - c], fw_s, fw_r)

    def hidden_grads(h, core):
        @pl.loop(0, SPAN // TILE)
        def _(step):
            at = pl.ds(pl.multiple_of(step * TILE, TILE), TILE)
            z = jnp.dot(kin[h, core, at, :], wb13[h], preferred_element_type=F32)
            dh = lax.dot_general(din[h, core, at, :], wb2[h], NT, preferred_element_type=F32)
            z1, z3 = z[:, :HALF], z[:, HALF:]
            sg = 1.0 / (1.0 + jnp.exp(-z1))
            act = z1 * sg
            hid[core, at, :] = (act * z3).astype(BF)
            dz[core, at, :HALF] = (dh * z3 * sg * (1.0 + z1 * (1.0 - sg))).astype(BF)
            dz[core, at, HALF:] = (dh * act).astype(BF)

    def block(j, rows, start=0, count=None):
        return pl.ds(pl.multiple_of(lax.rem(y + j, 4) * rows + start, 16), count or rows)

    def send_y(gs, ra, ry, n, i):
        k = n // 2
        remote(gs.at[block(2, n, 0, k)], ra.at[0], ry_s.at[i], ra_r.at[i], tok=up).start()
        remote(gs.at[block(2, n, k, k)], ra.at[1], ry_s.at[i], ra_r.at[i], tok=down).start()
        remote(gs.at[block(1, n, k, k)], ry.at[0], ry_s.at[i], ry_r.at[i], tok=up).start()
        remote(gs.at[block(3, n, 0, k)], ry.at[1], ry_s.at[i], ry_r.at[i], tok=down).start()
        pending["ra", i] = (ra, ra_r.at[i])

    def weight_grads(h):
        g = lax.dot_general(kin[h, 0], dz[0], TN, preferred_element_type=F32)
        g += lax.dot_general(kin[h, 1], dz[1], TN, preferred_element_type=F32)
        gs13[h] = g.astype(BF)
        send_y(gs13.at[h], ra13.at[h], ry13.at[h], 128, 2 * h)
        g = lax.dot_general(hid[0], din[h, 0], TN, preferred_element_type=F32)
        g += lax.dot_general(hid[1], din[h, 1], TN, preferred_element_type=F32)
        gs2[h] = g.astype(BF)
        send_y(gs2.at[h], ra2.at[h], ry2.at[h], 64, 2 * h + 1)

    mats = (
        (gs13, ra13, rb13, ry13, py13, zs13, rz13, gg13, 128),
        (gs2, ra2, rb2, ry2, py2, zs2, rz2, gg2, 64),
    )

    def relay_y(h):
        for i, (gs, ra, rb, ry, py, zs, rz, gg, n) in enumerate(mats):
            j, k = 2 * h + i, n // 2
            done("ra", j)
            rb[h, 0] = (gs[h, block(1, n, 0, k), :].astype(F32) + ra[h, 0].astype(F32)).astype(BF)
            rb[h, 1] = (gs[h, block(3, n, k, k), :].astype(F32) + ra[h, 1].astype(F32)).astype(BF)
            remote(rb.at[h, 0], ry.at[h, 2], ry_s.at[j], ry_r.at[j], tok=up).start()
            remote(rb.at[h, 1], ry.at[h, 3], ry_s.at[j], ry_r.at[j], tok=down).start()
            track("ry", j, gs.at[h, pl.ds(0, 3 * n)], ry.at[h], ry_s, ry_r)

    def reduce_y(h):
        for i, (gs, ra, rb, ry, py, zs, rz, gg, n) in enumerate(mats):
            j, k = 2 * h + i, n // 2
            done("ry", j)
            own = gs[h, block(0, n), :].astype(F32)
            py[h, :k, :] = own[:k] + (ry[h, 2].astype(F32) + ry[h, 1].astype(F32))
            py[h, k:, :] = own[k:] + (ry[h, 0].astype(F32) + ry[h, 3].astype(F32))
            zs[h] = py[h, pl.ds(pl.multiple_of((1 - zh) * k, k), k), :].astype(BF)
            remote(zs.at[h], rz.at[h], rz_s.at[j], rz_r.at[j], tok=zpeer).start()
            track("rz", j, zs.at[h], rz.at[h], rz_s, rz_r)

    def piece(gg, h, j, n, e):
        k = n // 2
        return gg.at[h, c, pl.ds(pl.multiple_of(lax.rem(y + j, 4) * n + e * k, k), k)]

    def gather(h):
        for i, (gs, ra, rb, ry, py, zs, rz, gg, n) in enumerate(mats):
            j, k = 2 * h + i, n // 2
            done("rz", j)
            total = py[h, pl.ds(pl.multiple_of(zh * k, k), k), :] + rz[h].astype(F32)
            view = piece(gg, h, 0, n, zh)
            view[...] = total.astype(BF)
            remote(view, view, az_s.at[j], az_r.at[j], tok=zpeer).start()
            remote(view, view, ay_s.at[j], au_r.at[j], tok=up).start()
            remote(view, view, ay_s.at[j], ay_r.at[j], tok=down).start()
            track("az", j, view, piece(gg, h, 0, n, 1 - zh), az_s, az_r)

    def pass_on(h):
        for i, (gs, ra, rb, ry, py, zs, rz, gg, n) in enumerate(mats):
            j = 2 * h + i
            done("az", j)
            view = piece(gg, h, 0, n, 1 - zh)
            remote(view, view, ay_s.at[j], ad_r.at[j], tok=down).start()
            remote(view, view, ay_s.at[j], ay_r.at[j], tok=up).start()

    def relay_gather(h):
        for i, (gs, ra, rb, ry, py, zs, rz, gg, n) in enumerate(mats):
            j = 2 * h + i
            for sem, near, e, to in ((au_r, 3, zh, up), (ad_r, 1, 1 - zh, down)):
                view = piece(gg, h, near, n, e)
                pltpu.make_async_copy(view, view, sem.at[j]).wait()
                remote(view, view, ay_s.at[j], ay_r.at[j], tok=to).start()
            three = gg.at[h, c, pl.ds(0, 3 * n)]
            track("ay", j, three, gg.at[h, c, pl.ds(0, 2 * n)], ay_s, ay_r)

    def share(h):
        done("ay", 2 * h)
        mine = gg13.at[h, c, :, pl.ds(pl.multiple_of((1 - c) * HALF, HALF), HALF)]
        theirs = gg13.at[h, 1 - c, :, half]
        remote(mine, mine, fg_s.at[2 * h], fg_r.at[2 * h], tok=sib).start()
        track("fg", 2 * h, mine, theirs, fg_s, fg_r)
        done("ay", 2 * h + 1)
        remote(gg2.at[h, c], gg2.at[h, c], fg_s.at[2 * h + 1], fg_r.at[2 * h + 1], tok=sib).start()
        track("fg", 2 * h + 1, gg2.at[h, c], gg2.at[h, 1 - c], fg_s, fg_r)

    outs = (out1, out3, out2)

    def newton(parts):
        squares = jnp.sum(parts[0] ** 2) + jnp.sum(parts[1] ** 2)
        scale = 1.0 / (jnp.sqrt(jnp.full((8, 128), squares, F32)) + 1e-06)
        scale = scale[:1, :1]
        for part in range(2):
            piece_ = parts[part] * scale
            where = pl.ds(part * HALF, HALF)
            if parts[part].shape[0] == HALF:
                xs[where, :] = piece_
                xb[0, where, :] = piece_.astype(BF)
            else:
                xs[:, where] = piece_
                xb[0, :, where] = piece_.astype(BF)
        for step in range(ITERS):
            now, later = step % 2, (step + 1) % 2
            square = lax.dot_general(xb[now], xb[now], NT, preferred_element_type=F32)
            cube = jnp.dot(square.astype(BF), xb[now], preferred_element_type=F32)
            fresh = 1.5 * xs[...] - 0.5 * cube
            if step < ITERS - 1:
                xs[...] = fresh
                xb[later] = fresh.astype(BF)
        return fresh

    def renew(h, m, ortho):
        update = wv[m, h] - ortho
        new_norm = jnp.sqrt(jnp.sum(update * update, axis=0, keepdims=True) + 1e-06)
        fresh = update * (oldn[h, m, :1, :] / new_norm)
        nf[h, m] = fresh
        nb[m] = fresh.astype(BF)

    def newton_own(h):
        done("fg", 2 * h)
        xf[h, c] = newton([gg13[h, part, :, half].astype(F32) for part in range(2)]).astype(BF)
        remote(xf.at[h, c], xf.at[h, c], xf_s.at[h], xf_r.at[h], tok=sib).start()
        track("xf", h, xf.at[h, c], xf.at[h, 1 - c], xf_s, xf_r)

    def newton_second(h):
        done("fg", 2 * h + 1)
        renew(h, 2, newton([gg2[h, part].astype(F32) for part in range(2)]))

    def renew_both(h):
        renew(h, c, xf[h, c].astype(F32))
        done("xf", h)
        renew(h, 1 - c, xf[h, 1 - c].astype(F32))
        for m in range(3):
            sem = nf_sem.at[3 * h + m]
            pltpu.make_async_copy(nf.at[h, m], outs[m].at[h], sem).start()
            pending["nf_s", 3 * h + m] = (nf.at[h, m], sem)

    def apply(h):
        done("a2a", 4 + h)

        for tile in range(SPAN // TILE):
            at = pl.ds(tile * TILE, TILE)
            q = qin[h, at, :]
            y1 = jnp.dot(q, nb[0], preferred_element_type=F32)
            y3 = jnp.dot(q, nb[1], preferred_element_type=F32)
            qh[...] = (y1 * (1.0 / (1.0 + jnp.exp(-y1))) * y3).astype(BF)
            ov[h, at, :] = jnp.dot(qh[...], nb[2], preferred_element_type=F32).astype(BF)
            for i in range(tile * TILE // ROWS, (tile + 1) * TILE // ROWS):
                land = mixed.at[:, columns(hi, h)]
                if i == OWN:
                    pltpu.make_async_copy(ov.at[h, slot(i)], land, o_r.at[h]).start()
                else:
                    remote(ov.at[h, slot(i)], land, o_s.at[h], o_r.at[h], head=peers[i]).start()
        track("out", h, ov.at[h, pl.ds(0, SPAN - ROWS)], ov.at[h], o_s, o_r)

    def arrived(name, h):
        done(name, 2 * h)
        done(name, 2 * h + 1)

    steps = [
        lambda: forward(0),
        lambda: hidden_grads(0, c),
        lambda: arrived("fw", 0),
        lambda: hidden_grads(0, 1 - c),
        lambda: weight_grads(0),
        lambda: relay_y(0),
        lambda: forward(1),
        lambda: scatter(q_hbm, qin.at[0], 4 + 0, 0),
        lambda: hidden_grads(1, c),
        lambda: reduce_y(0),
        lambda: arrived("fw", 1),
        lambda: hidden_grads(1, 1 - c),
        lambda: weight_grads(1),
        lambda: gather(0),
        lambda: relay_y(1),
        lambda: reduce_y(1),
        lambda: pass_on(0),
        lambda: relay_gather(0),
        lambda: gather(1),
        lambda: pass_on(1),
        lambda: share(0),
        lambda: relay_gather(1),
        lambda: newton_own(0),
        lambda: share(1),
        lambda: scatter(q_hbm, qin.at[1], 4 + 1, 1),
        lambda: newton_second(0),
        lambda: renew_both(0),
        lambda: apply(0),
        lambda: newton_own(1),
        lambda: newton_second(1),
        lambda: renew_both(1),
        lambda: apply(1),
    ]
    for step in steps:
        step()

    for key in sorted(pending, key=lambda key: (key[0].endswith("_s"), key)):
        done(*key)


def hand_out(*refs):
    ins, outs, held, in_sem, out_sem = refs[:4], refs[4:8], refs[8:12], refs[12], refs[13]
    parts = [(i, 0, row) for i in (1, 2, 3) for row in (0, HALF)]
    parts += [(0, 0, 0)] + [(i, 1, row) for i in (1, 2, 3) for row in (0, HALF)]

    def view(i, ref, h, row):
        return ref.at[h, pl.ds(row, HALF)] if i else ref

    loads = [
        pltpu.make_async_copy(view(i, ins[i], h, r), view(i, held[i], h, r), in_sem.at[n])
        for n, (i, h, r) in enumerate(parts)
    ]
    stores = [
        pltpu.make_async_copy(view(i, held[i], h, r), view(i, outs[i], h, r), out_sem.at[n])
        for n, (i, h, r) in enumerate(parts)
    ]
    for load in loads:
        load.start()
    for load, store in zip(loads, stores):
        load.wait()
        store.start()
    for store in stores:
        store.wait()


def on_device(queries, keys, values, rates, w_first, w_gate, w_second):
    any_spec = pl.BlockSpec(memory_space=pl.ANY)
    dma = pltpu.SemaphoreType.DMA
    weights = jax.ShapeDtypeStruct(w_first.shape, F32)
    vm = pltpu.VMEM
    results = pl.pallas_call(
        kernel,
        out_shape=(jax.ShapeDtypeStruct(queries.shape, BF), weights, weights, weights),
        in_specs=[any_spec] * 7,
        out_specs=[any_spec] * 4,
        scratch_shapes=[
            vm((3, 2, DH, DH), F32),
            vm(values.shape, BF),
            vm(rates.shape[::-1], BF),
            vm(values.shape, BF),
            vm((2, 2, SPAN, DH), BF),
            vm((2, 2, SPAN, DH), BF),
            vm((2, SPAN, DH), BF),
            vm((2, DH, DH), BF),
            vm((2, HALF, DH), BF),
            vm((2, 3, 8, DH), F32),
            vm((2, SPAN, DH), BF),
            vm((2, SPAN, HALF), BF),
            vm((2, DH, DH), BF),
            vm((2, HALF, DH), BF),
            vm((2, 2, 64, DH), BF),
            vm((2, 2, 32, DH), BF),
            vm((2, 2, 64, DH), BF),
            vm((2, 2, 32, DH), BF),
            vm((2, 4, 64, DH), BF),
            vm((2, 4, 32, DH), BF),
            vm((2, 128, DH), F32),
            vm((2, 64, DH), F32),
            vm((2, 64, DH), BF),
            vm((2, 32, DH), BF),
            vm((2, 64, DH), BF),
            vm((2, 32, DH), BF),
            vm((2, 2, DH, DH), BF),
            vm((2, 2, HALF, DH), BF),
            vm((DH, DH), F32),
            vm((2, DH, DH), BF),
            vm((2, 2, DH, DH), BF),
            vm((3, DH, DH), BF),
            vm((TILE, DH), BF),
            vm((2, SPAN, DH), BF),
            vm((2, 3, DH, DH), F32),
            dma((5,)), dma((6,)), dma((6,)), dma((4,)), dma((4,)), dma((4,)), dma((4,)), dma((4,)),
            dma((4,)), dma((4,)), dma((4,)), dma((4,)), dma((4,)), dma((4,)), dma((4,)), dma((4,)),
            dma((4,)), dma((4,)), dma((2,)), dma((2,)), dma((2,)), dma((2,)), dma((6,)),
        ],
        compiler_params=pltpu.CompilerParams(
            collective_id=0, has_side_effects=True, vmem_limit_bytes=VMEM_BYTES
        ),
        name="layer",
    )(queries, keys, values, rates.T, w_first, w_gate, w_second)
    return pl.pallas_call(
        hand_out,
        out_shape=(jax.ShapeDtypeStruct(queries.shape, BF), weights, weights, weights),
        in_specs=[any_spec] * 4,
        out_specs=[any_spec] * 4,
        scratch_shapes=[vm(queries.shape, BF)] + [vm(w_first.shape, F32)] * 3 + [dma((13,)), dma((13,))],
        compiler_params=pltpu.CompilerParams(vmem_limit_bytes=VMEM_BYTES),
        name="hand_out",
    )(*results)


def solution(mesh):
    placed = (
        P(("head", "tok"), None),
        P(("head", "tok"), None),
        P(("head", "tok"), None),
        P(("head", "tok"), None),
        P("head", None, None),
        P("head", None, None),
        P("head", None, None),
    )
    return jax.shard_map(
        on_device,
        mesh=mesh,
        in_specs=placed,
        out_specs=(
            P(("head", "tok"), None),
            P("head", None, None),
            P("head", None, None),
            P("head", None, None),
        ),
        check_vma=False,
    )
```
